256 devices in a mesh: grid: 32 (over x, z), mesh: 8 (over y, core).
Axes of the slice: x: 4, y: 4, z: 8, core: 2. Of those that a mesh axis runs over, the one named last changes fastest.
Arguments:
- grid_lat: bfloat16 [262144, 512], P(('grid', 'mesh')), may hold values from -6 to 6
- mesh_lat: bfloat16 [32768, 512], P(('grid', 'mesh')), may hold values from -6 to 6
- edge_grid_block: int32 [4096], P(('grid', 'mesh')), may hold values from 0 to 63, as said below
- edge_mesh_block: int32 [4096], P(('grid', 'mesh')), may hold values from 0 to 31
- edge_sender: int32 [1048576], P(('grid', 'mesh')), may hold values from 0 to 127
- edge_receiver: int32 [1048576], P(('grid', 'mesh')), may hold values from 0 to 127
- edge_live: int32 [4096], P(('grid', 'mesh')), may hold values from 64 to 256
- weight_in: bfloat16 [512, 512], replicated, may hold values from -0.25 to 0.25
- bias_in: float32 [512], replicated, may hold values from -3 to 3
- weight_out: bfloat16 [512, 512], replicated, may hold values from -0.25 to 0.25
- norm_gain: float32 [512], replicated, may hold values from 0.1 to 1.9
- weight_node: bfloat16 [512, 512], replicated, may hold values from -0.25 to 0.25
- cotangent: bfloat16 [32768, 512], P(('grid', 'mesh')), may hold values from -6 to 6
Outputs:
- mesh_out: bfloat16 [32768, 512], P(('grid', 'mesh'))
- grid_grad: bfloat16 [262144, 512], P(('grid', 'mesh'))
- grad_in: float32 [512, 512], replicated
- grad_out: float32 [512, 512], replicated
- grad_node: float32 [512, 512], replicated
The draws below stay inside these ranges and needn't reach their ends.
Inputs may be any that keep to these rules, and one draw needn't show every extreme that they name: `edge_grid_block`: within each aligned run of 16 entries the values are distinct, at most 4 of them share one value of v // 8, and in every run exactly 4 share some value of v // 8.
All inputs are finite; a program needn't handle non-finite values.
Results may differ from the reference program's by a relative error of at most 0.018.
Values may be sent and summed in bfloat16 or wider, within the bound.
No kernel may reach another device: no remote copies, remote signals or barrier semaphores. Data moves between devices by JAX's collectives and lax.ppermute only.
A program may use at most 128 MiB of HBM per device.

```python
import math
import jax
import jax.numpy as jnp
from jax import lax

D = 512
BLOCK = 128
GB_DEV = 8
EB_DEV = 16
EPB = 256
CAP = 4
BANDS = 8
OWNERS = 32
NG = 262144
NEB = 4096
EDGES = 1048576
MESH_NODES = 32768


def draw_edge_grid_block(key, part):
    key = jax.random.fold_in(key, 11)
    device_count = NEB // EB_DEV

    def one_device(device_key):
        sub_keys = jax.random.split(device_key, 4)
        ordering = jax.random.permutation(sub_keys[0], BANDS).astype(jnp.int32)
        others = jnp.repeat(ordering[1:], CAP, total_repeat_length=(BANDS - 1) * CAP)
        shuffled = jax.random.permutation(sub_keys[1], others)
        holders = jnp.concatenate([jnp.full((CAP,), ordering[0], jnp.int32), shuffled[:EB_DEV - CAP].astype(jnp.int32)])
        holders = holders[jax.random.permutation(sub_keys[2], EB_DEV)]
        same_holder = holders[:, None] == holders[None, :]
        position = jnp.arange(EB_DEV, dtype=jnp.int32)
        earlier = position[None, :] < position[:, None]
        ranking = jnp.sum(same_holder & earlier, axis=1).astype(jnp.int32)
        picks = jax.vmap(lambda block_key: jax.random.permutation(block_key, GB_DEV))(jax.random.split(sub_keys[3], BANDS))
        return (holders * GB_DEV + picks[holders, ranking]).astype(jnp.int32)
    return jax.vmap(one_device)(jax.random.split(key, device_count)).reshape(NEB)


def draw_edge_live(key, part):
    key = jax.random.fold_in(key, 23)
    sub_keys = jax.random.split(key, 2)
    counts = jax.random.randint(sub_keys[0], (NEB,), EPB // 4, EPB + 1)
    where_full = jax.random.randint(sub_keys[1], (), 0, NEB)
    return counts.at[where_full].set(EPB).astype(jnp.int32)


def set_ends(entries, own_key, low, largest):
    extent = entries.shape
    place = [jax.random.randint(jax.random.fold_in(own_key, axis), (), 0, extent[axis]) for axis in range(len(extent))]
    entries = entries.at[tuple(place)].set(low)
    longest = extent.index(max(extent))
    place[longest] = (place[longest] + 1) % extent[longest]
    return entries.at[tuple(place)].set(largest)


def steps_of(rng, extent, pieces, low, largest):
    level, own = 1.0, jax.random.fold_in(rng, 6)
    for axis_at, blocks in pieces:
        heights = jnp.exp(jax.random.uniform(jax.random.fold_in(own, axis_at), (blocks,), jnp.float32, low / len(pieces), largest / len(pieces)))
        level = level * jnp.repeat(heights, extent[axis_at] // blocks).reshape([-1 if axis == axis_at else 1 for axis in range(len(extent))])
    return level


def gaussian(rng, extent, spread, most, cuts=(), kind=jnp.bfloat16):
    gain = steps_of(rng, extent, cuts, -0.22, 0.18) if cuts else 1.0
    result = jax.random.normal(rng, extent, jnp.float32) * spread * gain
    return jnp.minimum(jnp.maximum(result, -most), most).astype(kind)


def setup_inputs(seed: int = 0) -> dict:
    arg_keys = jax.random.split(jax.random.key(seed), 14)
    grid_lat = gaussian(arg_keys[0], (NG, D), 1.0, 6.0, ((0, 256),))
    mesh_lat = gaussian(arg_keys[1], (MESH_NODES, D), 1.0, 6.0, ((0, 256),))
    edge_grid_block = draw_edge_grid_block(jax.random.fold_in(arg_keys[13], 71), 0)
    edge_mesh_block = set_ends(jax.random.randint(arg_keys[3], (NEB,), 0, OWNERS), jax.random.fold_in(arg_keys[3], 1), 0, OWNERS - 1).astype(jnp.int32)
    edge_sender = set_ends(jax.random.randint(arg_keys[4], (EDGES,), 0, BLOCK), jax.random.fold_in(arg_keys[4], 1), 0, BLOCK - 1).astype(jnp.int32)
    edge_receiver = set_ends(jax.random.randint(arg_keys[5], (EDGES,), 0, BLOCK), jax.random.fold_in(arg_keys[5], 1), 0, BLOCK - 1).astype(jnp.int32)
    edge_live = draw_edge_live(jax.random.fold_in(arg_keys[13], 71), 0)
    weight_in = gaussian(arg_keys[7], (D, D), D ** -0.5, 0.25)
    bias_in = gaussian(arg_keys[8], (D,), 0.5, 3.0, (), jnp.float32)
    weight_out = gaussian(arg_keys[9], (D, D), D ** -0.5, 0.25)
    norm_gain = jnp.clip(1.0 + 0.18 * jax.random.normal(arg_keys[10], (D,), jnp.float32), 0.1, 1.9)
    weight_node = gaussian(arg_keys[11], (D, D), D ** -0.5, 0.25)
    cotangent = gaussian(arg_keys[12], (MESH_NODES, D), 1.0, 6.0, ((0, 256),))
    return dict(grid_lat=grid_lat, mesh_lat=mesh_lat, edge_grid_block=edge_grid_block, edge_mesh_block=edge_mesh_block, edge_sender=edge_sender, edge_receiver=edge_receiver, edge_live=edge_live, weight_in=weight_in, bias_in=bias_in, weight_out=weight_out, norm_gain=norm_gain, weight_node=weight_node, cotangent=cotangent)


epsilon = 1e-05

def silu_slope(values):
    gate_value = jax.nn.sigmoid(values)
    return gate_value * (1.0 + values * (1.0 - gate_value))

def node_forward(mesh_lat, aggregate, norm_gain, weight_node):
    summed = mesh_lat.astype(jnp.float32) + aggregate
    centred = summed - lax.optimization_barrier(jnp.mean(summed, axis=-1, keepdims=True))
    inverse = lax.rsqrt(lax.optimization_barrier(jnp.mean(centred * centred, axis=-1, keepdims=True)) + epsilon)
    standard = centred * inverse
    normed = standard * norm_gain
    active = jax.nn.silu(normed).astype(jnp.bfloat16)
    mesh_out = (summed + jnp.dot(active, weight_node, preferred_element_type=jnp.float32)).astype(jnp.bfloat16)
    return (standard, inverse, normed, active, mesh_out)

def node_backward(cotangent, standard, inverse, normed, norm_gain, weight_node):
    d_active = jnp.dot(cotangent, weight_node.T, preferred_element_type=jnp.float32)
    d_standard = d_active * silu_slope(normed) * norm_gain
    mean_first = lax.optimization_barrier(jnp.mean(d_standard, axis=-1, keepdims=True))
    mean_second = lax.optimization_barrier(jnp.mean(d_standard * standard, axis=-1, keepdims=True))
    return cotangent.astype(jnp.float32) + inverse * (d_standard - mean_first - standard * mean_second)

def reference(grid_lat, mesh_lat, edge_grid_block, edge_mesh_block, edge_sender, edge_receiver, edge_live, weight_in, bias_in, weight_out, norm_gain, weight_node, cotangent):
    feature_width = grid_lat.shape[1]
    devices = OWNERS * BANDS
    group_blocks = grid_lat.reshape(OWNERS, BANDS * GB_DEV, BLOCK, feature_width)
    grid_table = edge_grid_block.reshape(devices, EB_DEV)
    mesh_table = edge_mesh_block.reshape(devices, EB_DEV)
    sender_table = edge_sender.reshape(devices, EB_DEV, EPB)
    receiver_table = edge_receiver.reshape(devices, EB_DEV, EPB)
    live_table = jnp.arange(EPB, dtype=jnp.int32)[None, None, :] < edge_live.reshape(devices, EB_DEV)[:, :, None]

    def edge_forward(device):
        blocks_here = group_blocks[device // BANDS]
        sender_rows = blocks_here[grid_table[device][:, None], sender_table[device]]
        flat_rows = sender_rows.reshape(EB_DEV * EPB, feature_width)
        pre_act = jnp.dot(flat_rows, weight_in, preferred_element_type=jnp.float32) + bias_in
        hidden = jax.nn.silu(pre_act).astype(jnp.bfloat16)
        message = jnp.dot(hidden, weight_out, preferred_element_type=jnp.float32).astype(jnp.bfloat16)
        return (flat_rows, pre_act, hidden, message)

    def add_partial(device, aggregate):
        device = device.astype(jnp.int32)
        flat_rows, pre_act, hidden, message = edge_forward(device)
        message = message.reshape(EB_DEV, EPB, feature_width).astype(jnp.float32)
        weighted = jnp.where(live_table[device][:, :, None], message, jnp.zeros_like(message))
        partial_value = jnp.zeros((OWNERS, BLOCK, feature_width), jnp.float32).at[mesh_table[device][:, None], receiver_table[device]].add(weighted)
        rounded = lax.optimization_barrier(partial_value.astype(jnp.bfloat16)).astype(jnp.float32)
        band_index = device % BANDS
        current = lax.dynamic_index_in_dim(aggregate, band_index, axis=1, keepdims=False)
        return lax.dynamic_update_index_in_dim(aggregate, current + rounded, band_index, axis=1)
    aggregate = lax.fori_loop(0, devices, add_partial, jnp.zeros((OWNERS, BANDS, BLOCK, feature_width), jnp.float32))
    aggregate = aggregate.reshape(devices * BLOCK, feature_width)
    standard, inverse, normed, active, mesh_out = node_forward(mesh_lat, aggregate, norm_gain, weight_node)
    d_summed = node_backward(cotangent, standard, inverse, normed, norm_gain, weight_node)
    d_agg = d_summed.astype(jnp.bfloat16).reshape(OWNERS, BANDS, BLOCK, feature_width)
    node_sum = jnp.dot(active.T, cotangent, preferred_element_type=jnp.float32)

    def group_step(group_index):

        def band_step(band_index, state_carry):
            band_index = band_index.astype(jnp.int32)
            row_sums, in_sum, out_sum = state_carry
            device = group_index * BANDS + band_index
            flat_rows, pre_act, hidden, message = edge_forward(device)
            band_cot = lax.dynamic_index_in_dim(d_agg, band_index, axis=1, keepdims=False)
            picked = band_cot[mesh_table[device][:, None], receiver_table[device]]
            d_message = jnp.where(live_table[device][:, :, None], picked, jnp.zeros_like(picked)).reshape(EB_DEV * EPB, feature_width)
            out_sum = out_sum + jnp.dot(hidden.T, d_message, preferred_element_type=jnp.float32)
            d_hidden = jnp.dot(d_message, weight_out.T, preferred_element_type=jnp.float32)
            d_pre = (d_hidden * silu_slope(pre_act)).astype(jnp.bfloat16)
            in_sum = in_sum + jnp.dot(flat_rows.T, d_pre, preferred_element_type=jnp.float32)
            block_ids = jnp.arange(EB_DEV, dtype=jnp.int32)[:, None]
            row_tiles = jnp.zeros((EB_DEV, BLOCK, feature_width), jnp.float32).at[block_ids, sender_table[device]].add(d_pre.reshape(EB_DEV, EPB, feature_width).astype(jnp.float32))
            rounded = lax.optimization_barrier(row_tiles.astype(jnp.bfloat16)).astype(jnp.float32)
            row_sums = row_sums.at[grid_table[device]].add(rounded)
            return (row_sums, in_sum, out_sum)
        initial = (jnp.zeros((BANDS * GB_DEV, BLOCK, feature_width), jnp.float32), jnp.zeros((feature_width, feature_width), jnp.float32), jnp.zeros((feature_width, feature_width), jnp.float32))
        row_sums, in_sum, out_sum = lax.fori_loop(0, BANDS, band_step, initial)
        group_grad = jnp.dot(row_sums.reshape(BANDS * GB_DEV * BLOCK, feature_width).astype(jnp.bfloat16), weight_in.T, preferred_element_type=jnp.float32).astype(jnp.bfloat16)
        return (group_grad, in_sum, out_sum)
    group_grads, in_sums, out_sums = lax.map(group_step, jnp.arange(OWNERS, dtype=jnp.int32))
    grid_grad = group_grads.reshape(OWNERS * BANDS * GB_DEV * BLOCK, feature_width)
    grad_in = lax.optimization_barrier(jnp.sum(in_sums, axis=0)) / math.sqrt(EDGES)
    grad_out = lax.optimization_barrier(jnp.sum(out_sums, axis=0)) / math.sqrt(EDGES)
    grad_node = node_sum / math.sqrt(MESH_NODES)
    return (mesh_out, grid_grad, grad_in, grad_out, grad_node)
```

```python
import math

import jax
import jax.numpy as jnp
from jax import lax
from jax.experimental import pallas as pl
from jax.experimental.pallas import tpu as pltpu
from jax.sharding import PartitionSpec as P

EPSILON = 1e-05
F32, BF16 = jnp.float32, jnp.bfloat16
NX, NZ, NY = 4, 8, 4
GRID_N, MESH_N = NX * NZ, 2 * NY
HALF = 256
VMEM = pl.BlockSpec(memory_space=pltpu.VMEM)
SMEM = pl.BlockSpec(memory_space=pltpu.SMEM)


def kernel_params():
    return pltpu.CompilerParams(vmem_limit_bytes=40 * 1024 * 1024)


def send_y(v, k, c):
    pairs = [(m, ((m // 2 + k) % NY) * 2 + ((m % 2) ^ c)) for m in range(MESH_N)]
    return lax.ppermute(v, "mesh", pairs)


def send_x(v, k):
    return lax.ppermute(v, "grid", [(g, ((g // NZ + k) % NX) * NZ + g % NZ) for g in range(GRID_N)])


def send_z(v, k):
    return lax.ppermute(v, "grid", [(g, (g // NZ) * NZ + (g % NZ + k) % NZ) for g in range(GRID_N)])


def total(parts, dtype=BF16):
    t = parts[0].astype(F32)
    for p in parts[1:]:
        t = t + p.astype(F32)
    return t.astype(dtype)


def scatter_x(parts, dtype=BF16):
    return total([parts[0]] + [send_x(parts[k], k) for k in (2, 1, 3)], dtype)


def scatter_z_direct(parts, dtype=BF16):
    return total([parts[0]] + [send_z(parts[k], k) for k in (4, 3, 5, 2, 6, 1, 7)], dtype)


def scatter_z_ring(parts):
    up, down = send_z(parts[3], 1), send_z(parts[4], -1)
    up, down = total([up, parts[2]]), total([down, parts[5]])
    up, down = send_z(up, 1), send_z(down, -1)
    up, down = total([up, parts[1]]), total([down, parts[6]])
    up, down = send_z(up, 1), send_z(down, -1)
    down = send_z(total([down, parts[7]]), -1)
    return total([parts[0], up, down])


def gather_z_ring(v):
    out = [v] + [None] * (NZ - 1)
    up = down = v
    for k in range(1, 5):
        if k < 4:
            up = send_z(up, 1)
            out[NZ - k] = up
        down = send_z(down, -1)
        out[k] = down
    return out


def select_tile(index, arrays, size, write):
    which, place = index // size, index % size
    for a, ref in enumerate(arrays):

        @pl.when(which == a)
        def _():
            write(ref, place)


def edge_forward_kernel(tile, slot, *refs):
    xs = refs[:MESH_N]
    adj, w_in, bias = refs[MESH_N : MESH_N + 3]
    x_sel, slope, out0, out1, out2, out3, part = refs[MESH_N + 3 :]
    outs = (out0, out1, out2, out3)
    part[...] = jnp.zeros_like(part)
    count = adj.shape[0]

    def step(i, _):
        for r in range(2):
            j = 2 * i + r

            def write(ref, place):
                x_sel[j] = ref[place]

            select_tile(tile[j], xs, NZ, write)
        rows = x_sel[pl.ds(2 * i, 2)]
        rows = rows.reshape(2 * rows.shape[1], rows.shape[2])
        pre = jnp.dot(rows, w_in[...], preferred_element_type=F32) + bias[...]
        gate = jax.nn.sigmoid(pre)
        hidden = (pre * gate).astype(BF16)
        rise = (gate * (1.0 + pre * (1.0 - gate))).astype(BF16)
        for r in range(2):
            j = 2 * i + r
            slope[j] = rise[r * 128 : (r + 1) * 128]
            term = jnp.dot(adj[j], hidden[r * 128 : (r + 1) * 128], preferred_element_type=F32)
            part[slot[j]] += term
        return 0

    lax.fori_loop(0, count // 2, step, 0)
    for a in range(NX):
        outs[a][...] = part[a * NZ : (a + 1) * NZ].astype(BF16)


def edge_forward(tile, slot, xs, adj, w_in, bias):
    count, rows, width = adj.shape[0], xs[0].shape[1], xs[0].shape[2]
    block = jax.ShapeDtypeStruct((count, rows, width), BF16)
    dest = jax.ShapeDtypeStruct((NZ, rows, width), BF16)
    return pl.pallas_call(
        edge_forward_kernel,
        out_shape=(block, block) + (dest,) * NX,
        in_specs=[SMEM, SMEM] + [VMEM] * (MESH_N + 3),
        out_specs=(VMEM,) * (2 + NX),
        scratch_shapes=[pltpu.VMEM((GRID_N, rows, width), F32)],
        compiler_params=kernel_params(),
        name="edge_forward",
    )(tile, slot, *xs, adj, w_in, bias.reshape(1, -1))


def times_transposed(a, b):
    return lax.dot_general(a, b, (((1,), (1,)), ((), ())), preferred_element_type=F32)


def transposed_times(a, b):
    return lax.dot_general(a, b, (((0,), (0,)), ((), ())), preferred_element_type=F32)


def node_kernel(
    agg_a, agg_b, mesh_lat, cot, w_out, w_node, gain, mesh_out, u_a, u_b, active_out, agg_out, d_agg_out
):
    agg = jnp.concatenate([agg_a[...], agg_b[...]], axis=1)
    high = agg.astype(BF16)
    low = (agg - high.astype(F32)).astype(BF16)
    aggregate = jnp.dot(high, w_out[...], preferred_element_type=F32) + jnp.dot(
        low, w_out[...], preferred_element_type=F32
    )
    summed = mesh_lat[...].astype(F32) + aggregate
    centred = summed - jnp.mean(summed, axis=-1, keepdims=True)
    inverse = lax.rsqrt(jnp.mean(centred * centred, axis=-1, keepdims=True) + EPSILON)
    standard = centred * inverse
    normed = standard * gain[...]
    gate = jax.nn.sigmoid(normed)
    active = (normed * gate).astype(BF16)
    mesh_out[...] = (summed + jnp.dot(active, w_node[...], preferred_element_type=F32)).astype(BF16)
    d_active = times_transposed(cot[...], w_node[...])
    d_standard = d_active * (gate * (1.0 + normed * (1.0 - gate))) * gain[...]
    first = jnp.mean(d_standard, axis=-1, keepdims=True)
    second = jnp.mean(d_standard * standard, axis=-1, keepdims=True)
    d_summed = cot[...].astype(F32) + inverse * (d_standard - first - standard * second)
    d_agg = d_summed.astype(BF16)
    u = times_transposed(d_agg, w_out[...]).astype(BF16)
    u_a[...] = u[:, :HALF]
    u_b[...] = u[:, HALF:]
    active_out[...] = active
    agg_out[...] = high
    d_agg_out[...] = d_agg


def node_step(agg_a, agg_b, mesh_lat, cot, w_out, w_node, gain):
    rows, width = mesh_lat.shape
    whole = jax.ShapeDtypeStruct((rows, width), BF16)
    return pl.pallas_call(
        node_kernel,
        out_shape=(
            whole,
            jax.ShapeDtypeStruct((rows, HALF), BF16),
            jax.ShapeDtypeStruct((rows, width - HALF), BF16),
            whole,
            whole,
            whole,
        ),
        in_specs=[VMEM] * 7,
        out_specs=(VMEM,) * 6,
        compiler_params=kernel_params(),
        name="node_step",
    )(agg_a, agg_b, mesh_lat, cot, w_out, w_node, gain.reshape(1, -1))


def edge_backward_kernel(slot, flipped, out_place, *refs):
    u_a, u_b = refs[:NX], refs[NX : NX + NZ]
    adj, slope = refs[NX + NZ : NX + NZ + 2]
    d_pre = refs[NX + NZ + 2]
    outs = refs[NX + NZ + 3 : NX + NZ + 3 + MESH_N]
    u = refs[-1]
    count = adj.shape[0]

    def step(j, _):
        def write_a(ref, place):
            u[:, :HALF] = ref[place]

        def write_b(ref, place):
            u[:, HALF:] = ref[place]

        select_tile(slot[j], u_a, NZ, write_a)
        select_tile(flipped[j], u_b, NX, write_b)
        term = transposed_times(adj[j], u[...]) * slope[j].astype(F32)
        d_pre[j] = term.astype(BF16)

        def write_out(ref, place):
            ref[place] = d_pre[j]

        select_tile(out_place[j], outs, 4, write_out)
        return 0

    for ref in outs:
        ref[...] = jnp.zeros_like(ref)
    lax.fori_loop(0, count, step, 0)


def edge_backward(slot, flipped, out_place, u_a, u_b, adj, slope):
    count, rows, width = slope.shape
    return pl.pallas_call(
        edge_backward_kernel,
        out_shape=(jax.ShapeDtypeStruct(slope.shape, BF16),)
        + (jax.ShapeDtypeStruct((4, rows, width), BF16),) * MESH_N,
        in_specs=[SMEM] * 3 + [VMEM] * (NX + NZ + 2),
        out_specs=(VMEM,) * (1 + MESH_N),
        scratch_shapes=[pltpu.VMEM((rows, width), BF16)],
        compiler_params=kernel_params(),
        name="edge_backward",
    )(slot, flipped, out_place, *u_a, *u_b, adj, slope)


def row_kernel(place, *refs):
    parts = refs[:MESH_N]
    w_in, out, acc = refs[MESH_N:]
    acc[...] = jnp.zeros_like(acc)
    for s, ref in enumerate(parts):
        for q in range(4):

            @pl.when(place[s * 4 + q] >= 0)
            def _():
                acc[place[s * 4 + q]] += ref[q].astype(F32)

    blocks, rows, width = acc.shape
    for i in range(0, blocks, 2):
        row_sum = acc[i : i + 2].reshape(2 * rows, width).astype(BF16)
        out[i * rows : (i + 2) * rows] = times_transposed(row_sum, w_in[...]).astype(BF16)


def row_step(place, parts, w_in, blocks):
    _, rows, width = parts[0].shape
    return pl.pallas_call(
        row_kernel,
        out_shape=jax.ShapeDtypeStruct((blocks * rows, width), BF16),
        in_specs=[SMEM] + [VMEM] * (MESH_N + 1),
        out_specs=VMEM,
        scratch_shapes=[pltpu.VMEM((blocks, rows, width), F32)],
        compiler_params=kernel_params(),
        name="row_step",
    )(place, *parts, w_in)


def sum_everywhere(v):
    rows, width = v.shape
    v = lax.all_to_all(v.reshape(MESH_N, rows // MESH_N, width), "mesh", 0, 0)
    v = v.astype(F32).sum(0).astype(BF16)
    v = lax.all_to_all(v.reshape(GRID_N, rows // (MESH_N * GRID_N), width), "grid", 0, 0)
    v = v.astype(F32).sum(0).astype(BF16)
    v = lax.all_to_all(jnp.broadcast_to(v[None], (GRID_N, *v.shape)), "grid", 0, 0)
    v = v.reshape(rows // MESH_N, width)
    v = lax.all_to_all(jnp.broadcast_to(v[None], (MESH_N, *v.shape)), "mesh", 0, 0)
    return v.reshape(rows, width)


def shards(
    grid_lat,
    mesh_lat,
    edge_grid_block,
    edge_mesh_block,
    edge_sender,
    edge_receiver,
    edge_live,
    weight_in,
    bias_in,
    weight_out,
    norm_gain,
    weight_node,
    cotangent,
):
    block_rows, width = mesh_lat.shape
    local_blocks = grid_lat.shape[0] // block_rows
    edge_blocks = edge_grid_block.shape[0]
    slot_count = edge_sender.shape[0] // edge_blocks
    g, m = lax.axis_index("grid"), lax.axis_index("mesh")
    my_x, my_z, my_y, my_core = g // NZ, g % NZ, m // 2, m % 2

    own = grid_lat.reshape(local_blocks, block_rows, width)
    same = [own] + [None] * 3
    for k in (2, 1, 3):
        same[k] = send_y(own, -k, 0)
    other = [send_y(v, 0, 1) for v in same]
    xs = [v for pair in zip(same, other) for v in pair]

    holder, place = edge_grid_block // local_blocks, edge_grid_block % local_blocks
    rel_holder = ((holder // 2 - my_y) % NY) * 2 + ((holder % 2) ^ my_core)
    tile = rel_holder * local_blocks + place
    rel_x, rel_z = (edge_mesh_block // NZ - my_x) % NX, (edge_mesh_block % NZ - my_z) % NZ
    slot, flipped = rel_x * NZ + rel_z, rel_z * NX + rel_x
    earlier = jnp.arange(edge_blocks)[None, :] < jnp.arange(edge_blocks)[:, None]
    rank = jnp.sum((rel_holder[:, None] == rel_holder[None, :]) & earlier, axis=1).astype(jnp.int32)
    out_place = rel_holder * 4 + rank

    table = lax.all_gather(edge_grid_block, "mesh", axis=0)
    mine = (table // local_blocks == m)[:, :, None]
    order = jnp.cumsum(mine.astype(jnp.int32), axis=1) - 1
    hit = mine & (order == jnp.arange(4, dtype=jnp.int32))
    returned = jnp.sum(jnp.where(hit, (table % local_blocks)[:, :, None] + 1, 0), axis=1) - 1
    ids = jnp.arange(MESH_N, dtype=jnp.int32)
    source = ((my_y + ids // 2) % NY) * 2 + ((ids % 2) ^ my_core)
    returned = jnp.sum(
        jnp.where((source[:, None] == ids)[:, :, None], returned[None], 0), axis=1
    ).reshape(-1)

    sender = edge_sender.reshape(edge_blocks, slot_count)
    receiver = edge_receiver.reshape(edge_blocks, slot_count)
    lanes = jnp.arange(block_rows, dtype=jnp.int32)
    live = jnp.arange(slot_count, dtype=jnp.int32)[None, :] < edge_live[:, None]
    send_hot = (sender[:, :, None] == lanes).astype(BF16)
    receive_hot = ((receiver[:, :, None] == lanes) & live[:, :, None]).astype(BF16)
    adj = jnp.einsum("ker,ket->krt", receive_hot, send_hot, preferred_element_type=F32).astype(BF16)

    x_sel, slope, *parts = edge_forward(tile, slot, xs, adj, weight_in, bias_in)

    first = [p[..., :HALF] for p in parts]
    second = [jnp.stack([p[r, :, HALF:] for p in parts]) for r in range(NZ)]
    z_sums = scatter_z_ring(second)
    x_sums = scatter_x(first)
    agg_a = scatter_z_direct([x_sums[r] for r in range(NZ)], F32)
    agg_b = scatter_x([z_sums[r] for r in range(NX)], F32)

    mesh_out, u_a, u_b, active, agg, d_agg = node_step(
        agg_a, agg_b, mesh_lat, cotangent, weight_out, weight_node, norm_gain
    )

    u_a = jnp.stack([u_a] + [send_z(u_a, -k) for k in range(1, NZ)])
    u_b = jnp.stack([u_b] + [send_x(u_b, -k) for k in range(1, NX)])
    u_a = [u_a] + [send_x(u_a, -k) for k in range(1, NX)]
    u_b = gather_z_ring(u_b)

    d_pre, *back = edge_backward(slot, flipped, out_place, u_a, u_b, adj, slope)

    got = [back[0]] + [None] * (MESH_N - 1)
    for k in (2, 1, 3, 0):
        for c in range(2):
            if k or c:
                got[((NY - k) % NY) * 2 + c] = send_y(back[k * 2 + c], k, c)

    grid_grad = row_step(returned, got, weight_in, local_blocks)

    in_term = transposed_times(
        x_sel.reshape(edge_blocks * block_rows, width), d_pre.reshape(edge_blocks * block_rows, width)
    )
    node_term = transposed_times(active, cotangent)
    out_term = transposed_times(agg, d_agg)
    terms = jnp.concatenate([in_term, out_term, node_term], axis=1).astype(BF16)
    sums = sum_everywhere(terms).astype(F32)
    edge_total = edge_blocks * slot_count * GRID_N * MESH_N
    node_total = block_rows * GRID_N * MESH_N
    grad_in = sums[:, :width] / math.sqrt(edge_total)
    grad_out = sums[:, width : 2 * width] / math.sqrt(edge_total)
    grad_node = sums[:, 2 * width :] / math.sqrt(node_total)
    return (mesh_out, grid_grad, grad_in, grad_out, grad_node)


def solution(mesh):
    rows = P(("grid", "mesh"), None)
    line = P(("grid", "mesh"))
    return jax.shard_map(
        shards,
        mesh=mesh,
        in_specs=(rows, rows, line, line, line, line, line, P(), P(), P(), P(), P(), rows),
        out_specs=(rows, rows, P(), P(), P()),
        check_vma=False,
    )
```

```python
import math

import jax
import jax.numpy as jnp
from jax import lax
from jax.experimental import pallas as pl
from jax.experimental.pallas import tpu as pltpu
from jax.sharding import PartitionSpec as P

EPSILON = 1e-05
F32, BF16 = jnp.float32, jnp.bfloat16
NX, NZ, NY = 4, 8, 4
GRID_N, MESH_N = NX * NZ, 2 * NY
HALF = 256
VMEM = pl.BlockSpec(memory_space=pltpu.VMEM)
SMEM = pl.BlockSpec(memory_space=pltpu.SMEM)


def kernel_params():
    return pltpu.CompilerParams(vmem_limit_bytes=40 * 1024 * 1024)


def send_y(v, k, c):
    pairs = [(m, ((m // 2 + k) % NY) * 2 + ((m % 2) ^ c)) for m in range(MESH_N)]
    return lax.ppermute(v, "mesh", pairs)


def send_x(v, k):
    return lax.ppermute(v, "grid", [(g, ((g // NZ + k) % NX) * NZ + g % NZ) for g in range(GRID_N)])


def send_z(v, k):
    return lax.ppermute(v, "grid", [(g, (g // NZ) * NZ + (g % NZ + k) % NZ) for g in range(GRID_N)])


def total(parts, dtype=BF16):
    t = parts[0].astype(F32)
    for p in parts[1:]:
        t = t + p.astype(F32)
    return t.astype(dtype)


def join(*parts):
    return jnp.concatenate(parts, axis=0)


def scatter_x(parts, dtype=BF16):
    return total([parts[0]] + [send_x(parts[k], k) for k in (2, 1, 3)], dtype)


def scatter_x_twice(parts):
    h = parts[2].shape[0] // 2
    up, down = send_x(parts[2][:h], 1), send_x(parts[2][h:], -1)
    up = send_x(join(total([up, parts[1][:h]]), parts[1][h:]), 1)
    down = send_x(join(parts[3][:h], total([down, parts[3][h:]])), -1)
    return total([parts[0], up, down])


def scatter_z_twice(parts, dtype=BF16):
    n = parts[0].shape[0]
    far = send_z(parts[4], 4)
    up = send_z(join(parts[2], parts[3]), 2)
    down = send_z(join(parts[6], parts[5]), -2)
    up_one = send_z(total([parts[1], up[n:]]), 1)
    down_one = send_z(total([parts[7], down[n:]]), -1)
    return total([parts[0], far, up[:n], down[:n], up_one, down_one], dtype)


def gather_z_twice(v):
    n = v.shape[0]
    far, up, down = send_z(v, 4), send_z(v, 1), send_z(v, -1)
    up_two, down_two = send_z(join(v, up), 2), send_z(join(v, down), -2)
    return join(v, down, down_two, far, up_two[n:], up_two[:n], up)


def gather_x_twice(v):
    h = v.shape[0] // 2
    up, down = send_x(v, 1), send_x(v, -1)
    return [v, down, send_x(down[:h], -1), send_x(up[h:], 1), up]


def scatter_z_ring(parts):
    up, down = send_z(parts[3], 1), send_z(parts[4], -1)
    up, down = total([up, parts[2]]), total([down, parts[5]])
    up, down = send_z(up, 1), send_z(down, -1)
    up, down = total([up, parts[1]]), total([down, parts[6]])
    up, down = send_z(up, 1), send_z(down, -1)
    down = send_z(total([down, parts[7]]), -1)
    return total([parts[0], up, down])


def gather_z_ring(v):
    out = [v] + [None] * (NZ - 1)
    up = down = v
    for k in range(1, 5):
        if k < 4:
            up = send_z(up, 1)
            out[NZ - k] = up
        down = send_z(down, -1)
        out[k] = down
    return out


def select_tile(index, arrays, write):
    start = 0
    for ref in arrays:
        lo, hi = start, start + ref.shape[0]

        @pl.when((index >= lo) & (index < hi))
        def _():
            write(ref, index - lo)

        start = hi


def edge_forward_kernel(tile, slot, *refs):
    xs = refs[:MESH_N]
    adj, w_in, bias = refs[MESH_N : MESH_N + 3]
    x_sel, slope = refs[MESH_N + 3 : MESH_N + 5]
    outs = refs[MESH_N + 5 : -1]
    part = refs[-1]
    part[...] = jnp.zeros_like(part)
    count = adj.shape[0]

    def step(i, _):
        for r in range(2):
            j = 2 * i + r

            def write(ref, place):
                x_sel[j] = ref[place]

            select_tile(tile[j], xs, write)
        rows = x_sel[pl.ds(2 * i, 2)]
        rows = rows.reshape(2 * rows.shape[1], rows.shape[2])
        pre = jnp.dot(rows, w_in[...], preferred_element_type=F32) + bias[...]
        gate = jax.nn.sigmoid(pre)
        hidden = (pre * gate).astype(BF16)
        rise = (gate * (1.0 + pre * (1.0 - gate))).astype(BF16)
        for r in range(2):
            j = 2 * i + r
            slope[j] = rise[r * 128 : (r + 1) * 128]
            term = jnp.dot(adj[j], hidden[r * 128 : (r + 1) * 128], preferred_element_type=F32)
            part[slot[j]] += term
        return 0

    lax.fori_loop(0, count // 2, step, 0)
    for a in range(NX):
        outs[a][...] = part[a * NZ : (a + 1) * NZ, :, :HALF].astype(BF16)
    for r in range(NZ):
        for a in range(NX):
            outs[NX + r][a] = part[a * NZ + r, :, HALF:].astype(BF16)


def edge_forward(tile, slot, xs, adj, w_in, bias):
    count, rows, width = adj.shape[0], xs[0].shape[1], xs[0].shape[2]
    block = jax.ShapeDtypeStruct((count, rows, width), BF16)
    by_x = jax.ShapeDtypeStruct((NZ, rows, HALF), BF16)
    by_z = jax.ShapeDtypeStruct((NX, rows, width - HALF), BF16)
    return pl.pallas_call(
        edge_forward_kernel,
        out_shape=(block, block) + (by_x,) * NX + (by_z,) * NZ,
        in_specs=[SMEM, SMEM] + [VMEM] * (MESH_N + 3),
        out_specs=(VMEM,) * (2 + NX + NZ),
        scratch_shapes=[pltpu.VMEM((GRID_N, rows, width), F32)],
        compiler_params=kernel_params(),
        name="edge_forward",
    )(tile, slot, *xs, adj, w_in, bias.reshape(1, -1))


def times_transposed(a, b):
    return lax.dot_general(a, b, (((1,), (1,)), ((), ())), preferred_element_type=F32)


def transposed_times(a, b):
    return lax.dot_general(a, b, (((0,), (0,)), ((), ())), preferred_element_type=F32)


def node_kernel(
    agg_a, agg_b, mesh_lat, cot, w_out, w_node, gain, mesh_out, u_a, u_b, active_out, agg_out, d_agg_out
):
    agg = jnp.concatenate([agg_a[...], agg_b[...]], axis=1)
    high = agg.astype(BF16)
    low = (agg - high.astype(F32)).astype(BF16)
    aggregate = jnp.dot(high, w_out[...], preferred_element_type=F32) + jnp.dot(
        low, w_out[...], preferred_element_type=F32
    )
    summed = mesh_lat[...].astype(F32) + aggregate
    centred = summed - jnp.mean(summed, axis=-1, keepdims=True)
    inverse = lax.rsqrt(jnp.mean(centred * centred, axis=-1, keepdims=True) + EPSILON)
    standard = centred * inverse
    normed = standard * gain[...]
    gate = jax.nn.sigmoid(normed)
    active = (normed * gate).astype(BF16)
    mesh_out[...] = (summed + jnp.dot(active, w_node[...], preferred_element_type=F32)).astype(BF16)
    d_active = times_transposed(cot[...], w_node[...])
    d_standard = d_active * (gate * (1.0 + normed * (1.0 - gate))) * gain[...]
    first = jnp.mean(d_standard, axis=-1, keepdims=True)
    second = jnp.mean(d_standard * standard, axis=-1, keepdims=True)
    d_summed = cot[...].astype(F32) + inverse * (d_standard - first - standard * second)
    d_agg = d_summed.astype(BF16)
    u = times_transposed(d_agg, w_out[...]).astype(BF16)
    u_a[...] = u[:, :HALF]
    u_b[...] = u[:, HALF:]
    active_out[...] = active
    agg_out[...] = high
    d_agg_out[...] = d_agg


def node_step(agg_a, agg_b, mesh_lat, cot, w_out, w_node, gain):
    rows, width = mesh_lat.shape
    whole = jax.ShapeDtypeStruct((rows, width), BF16)
    return pl.pallas_call(
        node_kernel,
        out_shape=(
            whole,
            jax.ShapeDtypeStruct((rows, HALF), BF16),
            jax.ShapeDtypeStruct((rows, width - HALF), BF16),
            whole,
            whole,
            whole,
        ),
        in_specs=[VMEM] * 7,
        out_specs=(VMEM,) * 6,
        compiler_params=kernel_params(),
        name="node_step",
    )(agg_a, agg_b, mesh_lat, cot, w_out, w_node, gain.reshape(1, -1))


def edge_backward_kernel(slot, flipped, out_place, *refs):
    refs, outs, u = refs[: -MESH_N - 1], refs[-MESH_N - 1 : -1], refs[-1]
    *refs, adj, slope, d_pre = refs
    u_a, u_b = refs[:-NZ], refs[-NZ:]
    count = adj.shape[0]

    def step(j, _):
        def write_a(ref, place):
            u[:, :HALF] = ref[place]

        def write_b(ref, place):
            u[:, HALF:] = ref[place]

        select_tile(slot[j], u_a, write_a)
        select_tile(flipped[j], u_b, write_b)
        term = transposed_times(adj[j], u[...]) * slope[j].astype(F32)
        d_pre[j] = term.astype(BF16)

        def write_out(ref, place):
            ref[place] = d_pre[j]

        select_tile(out_place[j], outs, write_out)
        return 0

    for ref in outs:
        ref[...] = jnp.zeros_like(ref)
    lax.fori_loop(0, count, step, 0)


def edge_backward(slot, flipped, out_place, u_a, u_b, adj, slope):
    count, rows, width = slope.shape
    return pl.pallas_call(
        edge_backward_kernel,
        out_shape=(jax.ShapeDtypeStruct(slope.shape, BF16),)
        + (jax.ShapeDtypeStruct((4, rows, width), BF16),) * MESH_N,
        in_specs=[SMEM] * 3 + [VMEM] * (len(u_a) + len(u_b) + 2),
        out_specs=(VMEM,) * (1 + MESH_N),
        scratch_shapes=[pltpu.VMEM((rows, width), BF16)],
        compiler_params=kernel_params(),
        name="edge_backward",
    )(slot, flipped, out_place, *u_a, *u_b, adj, slope)


def row_kernel(place, *refs):
    parts = refs[:MESH_N]
    w_in, out, acc = refs[MESH_N:]
    acc[...] = jnp.zeros_like(acc)
    for s, ref in enumerate(parts):
        for q in range(4):

            @pl.when(place[s * 4 + q] >= 0)
            def _():
                acc[place[s * 4 + q]] += ref[q].astype(F32)

    blocks, rows, width = acc.shape
    for i in range(0, blocks, 2):
        row_sum = acc[i : i + 2].reshape(2 * rows, width).astype(BF16)
        out[i * rows : (i + 2) * rows] = times_transposed(row_sum, w_in[...]).astype(BF16)


def row_step(place, parts, w_in, blocks):
    _, rows, width = parts[0].shape
    return pl.pallas_call(
        row_kernel,
        out_shape=jax.ShapeDtypeStruct((blocks * rows, width), BF16),
        in_specs=[SMEM] + [VMEM] * (MESH_N + 1),
        out_specs=VMEM,
        scratch_shapes=[pltpu.VMEM((blocks, rows, width), F32)],
        compiler_params=kernel_params(),
        name="row_step",
    )(place, *parts, w_in)


def order_together(*values):
    return lax.optimization_barrier(values)


def pick(v, index):
    return lax.dynamic_index_in_dim(v, index, 0, keepdims=False)


def reduce_core(v, my_core):
    rows, width = v.shape
    v = v.reshape(2, rows // 2, width)
    return total([pick(v, my_core), send_y(pick(v, 1 - my_core), 0, 1)])


def reduce_y(v, my_y):
    rows, width = v.shape
    v = v.reshape(NY, rows // NY, width)
    parts = [pick(v, (my_y + k) % NY) for k in range(NY)]
    return total([parts[0]] + [send_y(parts[k], k, 0) for k in (2, 1, 3)])


def reduce_grid(v):
    rows, width = v.shape
    v = lax.all_to_all(v.reshape(GRID_N, rows // GRID_N, width), "grid", 0, 0)
    return v.astype(F32).sum(0).astype(BF16)


def spread_grid(v):
    rows, width = v.shape
    v = lax.all_to_all(jnp.broadcast_to(v[None], (GRID_N, rows, width)), "grid", 0, 0)
    return v.reshape(GRID_N * rows, width)


def spread_y(v, my_y):
    rows, width = v.shape
    got = [v] + [send_y(v, -k, 0) for k in (1, 2, 3)]
    whole = jnp.zeros((NY, rows, width), v.dtype)
    for k in range(NY):
        whole = lax.dynamic_update_slice(whole, got[k][None], ((my_y + k) % NY, 0, 0))
    return whole.reshape(NY * rows, width)


def spread_core(half, my_core):
    other = send_y(half, 0, 1)
    first = my_core == 0
    return jnp.concatenate([jnp.where(first, half, other), jnp.where(first, other, half)])


def shards(
    grid_lat,
    mesh_lat,
    edge_grid_block,
    edge_mesh_block,
    edge_sender,
    edge_receiver,
    edge_live,
    weight_in,
    bias_in,
    weight_out,
    norm_gain,
    weight_node,
    cotangent,
):
    block_rows, width = mesh_lat.shape
    local_blocks = grid_lat.shape[0] // block_rows
    edge_blocks = edge_grid_block.shape[0]
    slot_count = edge_sender.shape[0] // edge_blocks
    g, m = lax.axis_index("grid"), lax.axis_index("mesh")
    my_x, my_z, my_y, my_core = g // NZ, g % NZ, m // 2, m % 2

    own = grid_lat.reshape(local_blocks, block_rows, width)
    same = [own] + [None] * 3
    for k in (2, 1, 3):
        same[k] = send_y(own, -k, 0)
    other = [send_y(v, 0, 1) for v in same]
    xs = [v for pair in zip(same, other) for v in pair]

    holder, place = edge_grid_block // local_blocks, edge_grid_block % local_blocks
    rel_holder = ((holder // 2 - my_y) % NY) * 2 + ((holder % 2) ^ my_core)
    tile = rel_holder * local_blocks + place
    rel_x, rel_z = (edge_mesh_block // NZ - my_x) % NX, (edge_mesh_block % NZ - my_z) % NZ
    slot, flipped = rel_x * NZ + rel_z, rel_z * NX + rel_x
    earlier = jnp.arange(edge_blocks)[None, :] < jnp.arange(edge_blocks)[:, None]
    rank = jnp.sum((rel_holder[:, None] == rel_holder[None, :]) & earlier, axis=1).astype(jnp.int32)
    out_place = rel_holder * 4 + rank

    table = lax.all_gather(edge_grid_block, "mesh", axis=0)
    mine = (table // local_blocks == m)[:, :, None]
    order = jnp.cumsum(mine.astype(jnp.int32), axis=1) - 1
    hit = mine & (order == jnp.arange(4, dtype=jnp.int32))
    returned = jnp.sum(jnp.where(hit, (table % local_blocks)[:, :, None] + 1, 0), axis=1) - 1
    ids = jnp.arange(MESH_N, dtype=jnp.int32)
    source = ((my_y + ids // 2) % NY) * 2 + ((ids % 2) ^ my_core)
    returned = jnp.sum(
        jnp.where((source[:, None] == ids)[:, :, None], returned[None], 0), axis=1
    ).reshape(-1)

    sender = edge_sender.reshape(edge_blocks, slot_count)
    receiver = edge_receiver.reshape(edge_blocks, slot_count)
    lanes = jnp.arange(block_rows, dtype=jnp.int32)
    live = jnp.arange(slot_count, dtype=jnp.int32)[None, :] < edge_live[:, None]
    send_hot = (sender[:, :, None] == lanes).astype(BF16)
    receive_hot = ((receiver[:, :, None] == lanes) & live[:, :, None]).astype(BF16)
    adj = jnp.einsum("ker,ket->krt", receive_hot, send_hot, preferred_element_type=F32).astype(BF16)

    tile, returned = order_together(tile, returned)
    x_sel, slope, *parts = edge_forward(tile, slot, xs, adj, weight_in, bias_in)

    z_sums = scatter_z_ring(parts[NX:])
    x_sums = scatter_x_twice(parts[:NX])
    agg_a = scatter_z_twice([x_sums[r] for r in range(NZ)], F32)
    agg_b = scatter_x([z_sums[r] for r in range(NX)], F32)

    mesh_out, u_a, u_b, active, agg, d_agg = node_step(
        agg_a, agg_b, mesh_lat, cotangent, weight_out, weight_node, norm_gain
    )
    early = jnp.concatenate([transposed_times(agg, d_agg), transposed_times(active, cotangent)], axis=1)
    early = reduce_core(early.astype(BF16), my_core)

    u_b = jnp.stack([u_b] + [send_x(u_b, -k) for k in range(1, NX)])
    u_a = gather_z_twice(u_a).reshape(NZ, block_rows, HALF)
    u_a, early = order_together(u_a, early)
    early = reduce_y(early, my_y)
    u_a = gather_x_twice(u_a)
    u_b = gather_z_ring(u_b)
    slope, early = order_together(slope, early)

    d_pre, *back = edge_backward(slot, flipped, out_place, u_a, u_b, adj, slope)

    in_term = transposed_times(
        x_sel.reshape(edge_blocks * block_rows, width), d_pre.reshape(edge_blocks * block_rows, width)
    ).astype(BF16)

    got = [back[0]] + [None] * (MESH_N - 1)
    for k in (0, 2, 1, 3):
        for c in range(2):
            if k or c:
                got[((NY - k) % NY) * 2 + c] = send_y(back[k * 2 + c], k, c)
    sums = reduce_core(in_term, my_core)
    sums, got[1] = order_together(sums, got[1])
    sums = jnp.concatenate([reduce_y(sums, my_y), early], axis=1)
    sums, got[4] = order_together(sums, got[4])
    sums = reduce_grid(sums)
    sums, got[5] = order_together(sums, got[5])
    sums = spread_grid(sums)
    sums, got[6], got[2] = order_together(sums, got[6], got[2])
    sums = spread_y(sums, my_y)
    sums, got[7], got[3] = order_together(sums, got[7], got[3])
    sums = spread_core(sums, my_core).astype(F32)

    grid_grad = row_step(returned, got, weight_in, local_blocks)

    edge_total = edge_blocks * slot_count * GRID_N * MESH_N
    node_total = block_rows * GRID_N * MESH_N
    grad_in = sums[:, :width] / math.sqrt(edge_total)
    grad_out = sums[:, width : 2 * width] / math.sqrt(edge_total)
    grad_node = sums[:, 2 * width :] / math.sqrt(node_total)
    return (mesh_out, grid_grad, grad_in, grad_out, grad_node)


def solution(mesh):
    rows = P(("grid", "mesh"), None)
    line = P(("grid", "mesh"))
    return jax.shard_map(
        shards,
        mesh=mesh,
        in_specs=(rows, rows, line, line, line, line, line, P(), P(), P(), P(), P(), rows),
        out_specs=(rows, rows, P(), P(), P()),
        check_vma=False,
    )
```

```python
import math

import jax
import jax.numpy as jnp
from jax import lax
from jax.experimental import pallas as pl
from jax.experimental.pallas import tpu as pltpu
from jax.sharding import PartitionSpec as P

EPSILON = 1e-05
F32, BF16 = jnp.float32, jnp.bfloat16
NX, NZ, NY = 4, 8, 4
GRID_N, MESH_N = NX * NZ, 2 * NY
HALF = 256
VMEM = pl.BlockSpec(memory_space=pltpu.VMEM)
SMEM = pl.BlockSpec(memory_space=pltpu.SMEM)


def sigmoid(v):
    return 0.5 + 0.5 * jnp.tanh(0.5 * v)


def kernel_params():
    return pltpu.CompilerParams(vmem_limit_bytes=40 * 1024 * 1024)


def send_y(v, k, c):
    pairs = [(m, ((m // 2 + k) % NY) * 2 + ((m % 2) ^ c)) for m in range(MESH_N)]
    return lax.ppermute(v, "mesh", pairs)


def send_x(v, k):
    return lax.ppermute(v, "grid", [(g, ((g // NZ + k) % NX) * NZ + g % NZ) for g in range(GRID_N)])


def send_z(v, k):
    return lax.ppermute(v, "grid", [(g, (g // NZ) * NZ + (g % NZ + k) % NZ) for g in range(GRID_N)])


def order_together(*values):
    return lax.optimization_barrier(values)


def total(parts, dtype=BF16):
    t = parts[0].astype(F32)
    for p in parts[1:]:
        t = t + p.astype(F32)
    return t.astype(dtype)


def join(*parts):
    return jnp.concatenate(parts, axis=0)


def scatter_x(parts, dtype=BF16):
    return total([parts[0]] + [send_x(parts[k], k) for k in (2, 1, 3)], dtype)


def scatter_x_twice(parts):
    h = parts[2].shape[0] // 2
    up, down = send_x(parts[2][:h], 1), send_x(parts[2][h:], -1)
    up = send_x(join(total([up, parts[1][:h]]), parts[1][h:]), 1)
    down = send_x(join(parts[3][:h], total([down, parts[3][h:]])), -1)
    return total([parts[0], up, down])


def scatter_z_twice(parts, dtype=BF16):
    n = parts[0].shape[0]
    far = send_z(parts[4], 4)
    up = send_z(join(parts[2], parts[3]), 2)
    down = send_z(join(parts[6], parts[5]), -2)
    up_one = send_z(total([parts[1], up[n:]]), 1)
    down_one = send_z(total([parts[7], down[n:]]), -1)
    return total([parts[0], far, up[:n], down[:n], up_one, down_one], dtype)


def gather_z_twice(v):
    n = v.shape[0]
    up, down = send_z(v, 1), send_z(v, -1)
    late, up, down = order_together(v, up, down)
    far = send_z(late, 4)
    up_two, down_two = send_z(join(v, up), 2), send_z(join(v, down), -2)
    return join(v, down, down_two, far, up_two[n:], up_two[:n], up)


def gather_x_twice(v):
    h = v.shape[0] // 2
    up, down = send_x(v, 1), send_x(v, -1)
    return [v, down, send_x(down[:h], -1), send_x(up[h:], 1), up]


def scatter_z_ring(parts):
    up, down = send_z(parts[3], 1), send_z(parts[4], -1)
    up, down = total([up, parts[2]]), total([down, parts[5]])
    up, down = send_z(up, 1), send_z(down, -1)
    up, down = total([up, parts[1]]), total([down, parts[6]])
    up, down = send_z(up, 1), send_z(down, -1)
    down = send_z(total([down, parts[7]]), -1)
    return total([parts[0], up, down])


def gather_z_ring(v):
    out = [v] + [None] * (NZ - 1)
    up = down = v
    for k in range(1, 5):
        if k < 4:
            up = send_z(up, 1)
            out[NZ - k] = up
        down = send_z(down, -1)
        out[k] = down
    return out


def select_tile(index, arrays, write):
    start = 0
    for ref in arrays:
        lo, hi = start, start + ref.shape[0]

        @pl.when((index >= lo) & (index < hi))
        def _():
            write(ref, index - lo)

        start = hi


def edge_forward_kernel(tile, slot, *refs):
    xs = refs[:MESH_N]
    adj, w_in, bias = refs[MESH_N : MESH_N + 3]
    x_sel, slope = refs[MESH_N + 3 : MESH_N + 5]
    outs = refs[MESH_N + 5 : -1]
    part = refs[-1]
    part[...] = jnp.zeros_like(part)
    count = adj.shape[0]

    def step(i, _):
        for r in range(2):
            j = 2 * i + r

            def write(ref, place):
                x_sel[j] = ref[place]

            select_tile(tile[j], xs, write)
        rows = x_sel[pl.ds(2 * i, 2)]
        rows = rows.reshape(2 * rows.shape[1], rows.shape[2])
        pre = jnp.dot(rows, w_in[...], preferred_element_type=F32) + bias[...]
        gate = sigmoid(pre)
        hidden = (pre * gate).astype(BF16)
        rise = (gate * (1.0 + pre * (1.0 - gate))).astype(BF16)
        for r in range(2):
            j = 2 * i + r
            slope[j] = rise[r * 128 : (r + 1) * 128]
            term = jnp.dot(adj[j], hidden[r * 128 : (r + 1) * 128], preferred_element_type=F32)
            part[slot[j]] += term
        return 0

    lax.fori_loop(0, count // 2, step, 0, unroll=2)
    for a in range(NX):
        outs[a][...] = part[a * NZ : (a + 1) * NZ, :, :HALF].astype(BF16)
    for r in range(NZ):
        for a in range(NX):
            outs[NX + r][a] = part[a * NZ + r, :, HALF:].astype(BF16)


def edge_forward(tile, slot, xs, adj, w_in, bias):
    count, rows, width = adj.shape[0], xs[0].shape[1], xs[0].shape[2]
    block = jax.ShapeDtypeStruct((count, rows, width), BF16)
    by_x = jax.ShapeDtypeStruct((NZ, rows, HALF), BF16)
    by_z = jax.ShapeDtypeStruct((NX, rows, width - HALF), BF16)
    return pl.pallas_call(
        edge_forward_kernel,
        out_shape=(block, block) + (by_x,) * NX + (by_z,) * NZ,
        in_specs=[SMEM, SMEM] + [VMEM] * (MESH_N + 3),
        out_specs=(VMEM,) * (2 + NX + NZ),
        scratch_shapes=[pltpu.VMEM((GRID_N, rows, width), F32)],
        compiler_params=kernel_params(),
        name="edge_forward",
    )(tile, slot, *xs, adj, w_in, bias.reshape(1, -1))


def times_transposed(a, b):
    return lax.dot_general(a, b, (((1,), (1,)), ((), ())), preferred_element_type=F32)


def transposed_times(a, b):
    return lax.dot_general(a, b, (((0,), (0,)), ((), ())), preferred_element_type=F32)


def node_kernel(
    agg_a, agg_b, mesh_lat, cot, w_out, w_node, gain, mesh_out, u_a, u_b, active_out, agg_out, d_agg_out
):
    agg = jnp.concatenate([agg_a[...], agg_b[...]], axis=1)
    high = agg.astype(BF16)
    low = (agg - high.astype(F32)).astype(BF16)
    aggregate = jnp.dot(high, w_out[...], preferred_element_type=F32) + jnp.dot(
        low, w_out[...], preferred_element_type=F32
    )
    summed = mesh_lat[...].astype(F32) + aggregate
    centred = summed - jnp.mean(summed, axis=-1, keepdims=True)
    inverse = lax.rsqrt(jnp.mean(centred * centred, axis=-1, keepdims=True) + EPSILON)
    standard = centred * inverse
    normed = standard * gain[...]
    gate = sigmoid(normed)
    active = (normed * gate).astype(BF16)
    mesh_out[...] = (summed + jnp.dot(active, w_node[...], preferred_element_type=F32)).astype(BF16)
    d_active = times_transposed(cot[...], w_node[...])
    d_standard = d_active * (gate * (1.0 + normed * (1.0 - gate))) * gain[...]
    first = jnp.mean(d_standard, axis=-1, keepdims=True)
    second = jnp.mean(d_standard * standard, axis=-1, keepdims=True)
    d_summed = cot[...].astype(F32) + inverse * (d_standard - first - standard * second)
    d_agg = d_summed.astype(BF16)
    u = times_transposed(d_agg, w_out[...]).astype(BF16)
    u_a[...] = u[:, :HALF]
    u_b[...] = u[:, HALF:]
    active_out[...] = active
    agg_out[...] = high
    d_agg_out[...] = d_agg


def node_step(agg_a, agg_b, mesh_lat, cot, w_out, w_node, gain):
    rows, width = mesh_lat.shape
    whole = jax.ShapeDtypeStruct((rows, width), BF16)
    return pl.pallas_call(
        node_kernel,
        out_shape=(
            whole,
            jax.ShapeDtypeStruct((rows, HALF), BF16),
            jax.ShapeDtypeStruct((rows, width - HALF), BF16),
            whole,
            whole,
            whole,
        ),
        in_specs=[VMEM] * 7,
        out_specs=(VMEM,) * 6,
        compiler_params=kernel_params(),
        name="node_step",
    )(agg_a, agg_b, mesh_lat, cot, w_out, w_node, gain.reshape(1, -1))


def edge_backward_kernel(slot, flipped, out_place, *refs):
    refs, outs, (u_first, u_second, back) = refs[: -MESH_N - 3], refs[-MESH_N - 3 : -3], refs[-3:]
    *refs, adj, slope, d_pre = refs
    for scratch, pieces in ((u_first, refs[:-NZ]), (u_second, refs[-NZ:])):
        start = 0
        for ref in pieces:
            scratch[start : start + ref.shape[0]] = ref[...]
            start += ref.shape[0]

    def step(j, _):
        u = jnp.concatenate([u_first[slot[j]], u_second[flipped[j]]], axis=1)
        term = (transposed_times(adj[j], u) * slope[j].astype(F32)).astype(BF16)
        d_pre[j] = term
        back[out_place[j]] = term
        return 0

    lax.fori_loop(0, adj.shape[0], step, 0, unroll=4)
    for i, ref in enumerate(outs):
        ref[...] = back[4 * i : 4 * (i + 1)]


def edge_backward(slot, flipped, out_place, u_a, u_b, adj, slope):
    count, rows, width = slope.shape
    return pl.pallas_call(
        edge_backward_kernel,
        out_shape=(jax.ShapeDtypeStruct(slope.shape, BF16),)
        + (jax.ShapeDtypeStruct((4, rows, width), BF16),) * MESH_N,
        in_specs=[SMEM] * 3 + [VMEM] * (len(u_a) + len(u_b) + 2),
        out_specs=(VMEM,) * (1 + MESH_N),
        scratch_shapes=[
            pltpu.VMEM((GRID_N, rows, HALF), BF16),
            pltpu.VMEM((GRID_N, rows, width - HALF), BF16),
            pltpu.VMEM((4 * MESH_N, rows, width), BF16),
        ],
        compiler_params=kernel_params(),
        name="edge_backward",
    )(slot, flipped, out_place, *u_a, *u_b, adj, slope)


def row_kernel(place, *refs):
    parts = refs[:MESH_N]
    w_in, out, acc = refs[MESH_N:]
    acc[...] = jnp.zeros_like(acc)
    for s, ref in enumerate(parts):
        for q in range(4):

            @pl.when(place[s * 4 + q] >= 0)
            def _():
                acc[place[s * 4 + q]] += ref[q].astype(F32)

    blocks, rows, width = acc.shape
    for i in range(0, blocks, 2):
        row_sum = acc[i : i + 2].reshape(2 * rows, width).astype(BF16)
        out[i * rows : (i + 2) * rows] = times_transposed(row_sum, w_in[...]).astype(BF16)


def row_step(place, parts, w_in, blocks):
    _, rows, width = parts[0].shape
    return pl.pallas_call(
        row_kernel,
        out_shape=jax.ShapeDtypeStruct((blocks * rows, width), BF16),
        in_specs=[SMEM] + [VMEM] * (MESH_N + 1),
        out_specs=VMEM,
        scratch_shapes=[pltpu.VMEM((blocks, rows, width), F32)],
        compiler_params=kernel_params(),
        name="row_step",
    )(place, *parts, w_in)


def pick(v, index):
    return lax.dynamic_index_in_dim(v, index, 0, keepdims=False)


def reduce_core(v, my_core):
    rows, width = v.shape
    v = v.reshape(NY, 2, rows // MESH_N, width)
    keep = lax.dynamic_index_in_dim(v, my_core, 1, keepdims=False)
    return total([keep, send_y(lax.dynamic_index_in_dim(v, 1 - my_core, 1, keepdims=False), 0, 1)])


def reduce_y(v, my_y):
    parts = [pick(v, (my_y + k) % NY) for k in range(NY)]
    return total([parts[0]] + [send_y(parts[k], k, 0) for k in (2, 1, 3)])


def reduce_grid(v):
    rows, width = v.shape
    v = lax.all_to_all(v.reshape(GRID_N, rows // GRID_N, width), "grid", 0, 0)
    return v.astype(F32).sum(0).astype(BF16)


def spread_grid(v):
    rows, width = v.shape
    v = lax.all_to_all(jnp.broadcast_to(v[None], (GRID_N, rows, width)), "grid", 0, 0)
    return v.reshape(GRID_N * rows, width)


def spread_y(v):
    return jnp.stack([v] + [send_y(v, -k, 0) for k in (1, 2, 3)])


def finish_kernel(scales, me, mine, other, *outs):
    run = mine.shape[1]
    width = outs[0].shape[1]
    for k in range(NY):
        y = lax.rem(me[0] + k, NY)
        for ref, core in ((mine, me[1]), (other, 1 - me[1])):
            rows = pl.ds(pl.multiple_of((2 * y + core) * run, run), run)
            for i, out in enumerate(outs):
                out[rows, :] = ref[k, :, i * width : (i + 1) * width].astype(F32) * scales[i]


def finish(me, mine, other, width, scales):
    return pl.pallas_call(
        lambda *refs: finish_kernel(scales, *refs),
        out_shape=(jax.ShapeDtypeStruct((width, width), F32),) * 3,
        in_specs=[SMEM, VMEM, VMEM],
        out_specs=(VMEM,) * 3,
        compiler_params=kernel_params(),
        name="finish",
    )(me, mine, other)


def shards(
    grid_lat,
    mesh_lat,
    edge_grid_block,
    edge_mesh_block,
    edge_sender,
    edge_receiver,
    edge_live,
    weight_in,
    bias_in,
    weight_out,
    norm_gain,
    weight_node,
    cotangent,
):
    block_rows, width = mesh_lat.shape
    local_blocks = grid_lat.shape[0] // block_rows
    edge_blocks = edge_grid_block.shape[0]
    slot_count = edge_sender.shape[0] // edge_blocks
    g, m = lax.axis_index("grid"), lax.axis_index("mesh")
    my_x, my_z, my_y, my_core = g // NZ, g % NZ, m // 2, m % 2

    holder, place = edge_grid_block // local_blocks, edge_grid_block % local_blocks
    rel_holder = ((holder // 2 - my_y) % NY) * 2 + ((holder % 2) ^ my_core)
    tile = rel_holder * local_blocks + place
    rel_x, rel_z = (edge_mesh_block // NZ - my_x) % NX, (edge_mesh_block % NZ - my_z) % NZ
    slot, flipped = rel_x * NZ + rel_z, rel_z * NX + rel_x
    earlier = jnp.arange(edge_blocks)[None, :] < jnp.arange(edge_blocks)[:, None]
    rank = jnp.sum((rel_holder[:, None] == rel_holder[None, :]) & earlier, axis=1).astype(jnp.int32)
    out_place = rel_holder * 4 + rank

    own = grid_lat.reshape(local_blocks, block_rows, width)
    same = [own] + [None] * 3
    for k in (2, 1, 3):
        same[k] = send_y(own, -k, 0)
    other_own, blocks = order_together(send_y(own, 0, 1), edge_grid_block)

    table = jnp.stack([blocks] + [send_y(blocks, -k, 0) for k in (1, 2, 3)])
    table = jnp.stack([table, send_y(table, 0, 1)], axis=1).reshape(MESH_N, edge_blocks)
    mine = (table // local_blocks == m)[:, :, None]
    order = jnp.cumsum(mine.astype(jnp.int32), axis=1) - 1
    hit = mine & (order == jnp.arange(4, dtype=jnp.int32))
    returned = jnp.sum(jnp.where(hit, (table % local_blocks)[:, :, None] + 1, 0), axis=1) - 1
    returned = returned.reshape(-1)

    sender = edge_sender.reshape(edge_blocks, slot_count)
    receiver = edge_receiver.reshape(edge_blocks, slot_count)
    lanes = jnp.arange(block_rows, dtype=jnp.int32)
    live = jnp.arange(slot_count, dtype=jnp.int32)[None, :] < edge_live[:, None]
    send_hot = (sender[:, :, None] == lanes).astype(BF16)
    receive_hot = ((receiver[:, :, None] == lanes) & live[:, :, None]).astype(BF16)
    adj = jnp.einsum("ker,ket->krt", receive_hot, send_hot, preferred_element_type=F32).astype(BF16)

    same[1], adj, tile, slot, flipped, out_place, returned = order_together(
        same[1], adj, tile, slot, flipped, out_place, returned
    )
    other = [other_own] + [send_y(v, 0, 1) for v in same[1:]]
    xs = [v for pair in zip(same, other) for v in pair]

    x_sel, slope, *parts = edge_forward(tile, slot, xs, adj, weight_in, bias_in)

    z_sums = scatter_z_ring(parts[NX:])
    x_sums = scatter_x_twice(parts[:NX])
    agg_a = scatter_z_twice([x_sums[r] for r in range(NZ)], F32)
    agg_b = scatter_x([z_sums[r] for r in range(NX)], F32)

    mesh_out, u_a, u_b, active, agg, d_agg = node_step(
        agg_a, agg_b, mesh_lat, cotangent, weight_out, weight_node, norm_gain
    )
    u_b = jnp.stack([u_b] + [send_x(u_b, -k) for k in range(1, NX)])
    u_a = gather_z_twice(u_a).reshape(NZ, block_rows, HALF)
    u_a = gather_x_twice(u_a)
    u_b = gather_z_ring(u_b)

    d_pre, *back = edge_backward(slot, flipped, out_place, u_a, u_b, adj, slope)

    in_term = transposed_times(
        x_sel.reshape(edge_blocks * block_rows, width), d_pre.reshape(edge_blocks * block_rows, width)
    )
    node_term, out_term = transposed_times(active, cotangent), transposed_times(agg, d_agg)
    sums = jnp.concatenate([in_term, out_term, node_term], axis=1).astype(BF16)

    got = [back[0]] + [None] * (MESH_N - 1)
    for k in (0, 2, 1, 3):
        for c in range(2):
            if k or c:
                got[((NY - k) % NY) * 2 + c] = send_y(back[k * 2 + c], k, c)
    sums = reduce_core(sums, my_core)
    sums, got[1] = order_together(sums, got[1])
    sums = reduce_y(sums, my_y)
    sums, got[4] = order_together(sums, got[4])
    sums = reduce_grid(sums.reshape(-1, sums.shape[-1]))
    sums, got[5] = order_together(sums, got[5])
    sums = spread_grid(sums)
    sums, got[6], got[2] = order_together(sums, got[6], got[2])
    sums = spread_y(sums)
    sums, got[7], got[3] = order_together(sums, got[7], got[3])
    others = send_y(sums, 0, 1)

    grid_grad = row_step(returned, got, weight_in, local_blocks)

    by_edge = 1.0 / math.sqrt(edge_blocks * slot_count * GRID_N * MESH_N)
    by_node = 1.0 / math.sqrt(block_rows * GRID_N * MESH_N)
    me = jnp.stack([my_y, my_core]).astype(jnp.int32)
    grad_in, grad_out, grad_node = finish(me, sums, others, width, (by_edge, by_edge, by_node))
    return (mesh_out, grid_grad, grad_in, grad_out, grad_node)


def solution(mesh):
    rows = P(("grid", "mesh"), None)
    line = P(("grid", "mesh"))
    return jax.shard_map(
        shards,
        mesh=mesh,
        in_specs=(rows, rows, line, line, line, line, line, P(), P(), P(), P(), P(), rows),
        out_specs=(rows, rows, P(), P(), P()),
        check_vma=False,
    )
```

```python
import math

import jax
import jax.numpy as jnp
from jax import lax
from jax.experimental import pallas as pl
from jax.experimental.pallas import tpu as pltpu
from jax.sharding import PartitionSpec as P

EPSILON = 1e-05
F32, BF16 = jnp.float32, jnp.bfloat16
NX, NZ, NY = 4, 8, 4
GRID_N, MESH_N = NX * NZ, 2 * NY
HALF = 256
VMEM = pl.BlockSpec(memory_space=pltpu.VMEM)
SMEM = pl.BlockSpec(memory_space=pltpu.SMEM)


def sigmoid(v):
    return 0.5 + 0.5 * jnp.tanh(0.5 * v)


def kernel_params():
    return pltpu.CompilerParams(vmem_limit_bytes=40 * 1024 * 1024)


def send_y(v, k, c=0):
    pairs = [(m, ((m // 2 + k) % NY) * 2 + ((m % 2) ^ c)) for m in range(MESH_N)]
    return lax.ppermute(v, "mesh", pairs)


def send_x(v, k):
    return lax.ppermute(v, "grid", [(g, ((g // NZ + k) % NX) * NZ + g % NZ) for g in range(GRID_N)])


def send_z(v, k):
    return lax.ppermute(v, "grid", [(g, (g // NZ) * NZ + (g % NZ + k) % NZ) for g in range(GRID_N)])


def order_together(*values):
    return lax.optimization_barrier(values)


def total(parts, dtype=BF16):
    t = parts[0].astype(F32)
    for p in parts[1:]:
        t = t + p.astype(F32)
    return t.astype(dtype)


def join(*parts):
    return jnp.concatenate(parts, axis=0)


def scatter_x(parts, dtype=BF16):
    return total([parts[0]] + [send_x(parts[k], k) for k in (2, 1, 3)], dtype)


def scatter_x_twice(parts):
    h = parts[2].shape[0] // 2
    up, down = send_x(parts[2][:h], 1), send_x(parts[2][h:], -1)
    up = send_x(join(total([up, parts[1][:h]]), parts[1][h:]), 1)
    down = send_x(join(parts[3][:h], total([down, parts[3][h:]])), -1)
    return total([parts[0], up, down])


def scatter_z_twice(parts, dtype=BF16):
    n = parts[0].shape[0]
    far = send_z(parts[4], 4)
    up = send_z(join(parts[2], parts[3]), 2)
    down = send_z(join(parts[6], parts[5]), -2)
    up_one = send_z(total([parts[1], up[n:]]), 1)
    down_one = send_z(total([parts[7], down[n:]]), -1)
    return total([parts[0], far, up[:n], down[:n], up_one, down_one], dtype)


def gather_z_twice(v):
    n = v.shape[0]
    up, down = send_z(v, 1), send_z(v, -1)
    late, up, down = order_together(v, up, down)
    far = send_z(late, 4)
    up_two, down_two = send_z(join(v, up), 2), send_z(join(v, down), -2)
    v, down, down_two, far, up_two, up = order_together(v, down, down_two, far, up_two, up)
    return join(v, down, down_two, far, up_two[n:], up_two[:n], up)


def gather_x_twice(v):
    h = v.shape[0] // 2
    up, down = send_x(v, 1), send_x(v, -1)
    return [v, down, send_x(down[:h], -1), send_x(up[h:], 1), up]


def scatter_z_ring(parts):
    up, down = send_z(parts[3], 1), send_z(parts[4], -1)
    up, down = total([up, parts[2]]), total([down, parts[5]])
    up, down = send_z(up, 1), send_z(down, -1)
    up, down = total([up, parts[1]]), total([down, parts[6]])
    up, down = send_z(up, 1), send_z(down, -1)
    down = send_z(total([down, parts[7]]), -1)
    return total([parts[0], up, down])


def gather_z_ring(v):
    out = [v] + [None] * (NZ - 1)
    up = down = v
    for k in range(1, 5):
        if k < 4:
            up = send_z(up, 1)
            out[NZ - k] = up
        down = send_z(down, -1)
        out[k] = down
    return out


def lay_out(scratch, pieces):
    start = 0
    for ref in pieces:
        scratch[start : start + ref.shape[0]] = ref[...]
        start += ref.shape[0]


def edge_mlp(x, w_in, bias):
    pre = jnp.dot(x, w_in[...], preferred_element_type=F32) + bias[...]
    gate = sigmoid(pre)
    return (pre * gate).astype(BF16), (gate * (1.0 + pre * (1.0 - gate))).astype(BF16)


def edge_tiles(tile, first, xs, w_in, bias, x_sel, slope, hidden):
    count = sum(x.shape[0] for x in xs)

    def step(j, _):
        index = tile[j] - first

        @pl.when((index >= 0) & (index < count))
        def _():
            start = 0
            for x in xs:
                lo, hi = start, start + x.shape[0]

                @pl.when((index >= lo) & (index < hi))
                def _():
                    x_sel[j] = x[index - lo]

                start = hi
            hidden[j], slope[j] = edge_mlp(x_sel[j], w_in, bias)

        return 0

    lax.fori_loop(0, x_sel.shape[0], step, 0)


def edge_early_kernel(tile, *refs):
    *xs, w_in, bias, x_sel, slope, hidden = refs
    edge_tiles(tile, 0, xs, w_in, bias, x_sel, slope, hidden)


def edge_early(tile, xs, w_in, bias):
    count, rows, width = tile.shape[0], xs[0].shape[1], xs[0].shape[2]
    block = jax.ShapeDtypeStruct((count, rows, width), BF16)
    return pl.pallas_call(
        edge_early_kernel,
        out_shape=(block,) * 3,
        in_specs=[SMEM] + [VMEM] * (len(xs) + 2),
        out_specs=(VMEM,) * 3,
        compiler_params=kernel_params(),
        name="edge_early",
    )(tile, *xs, w_in, bias.reshape(1, -1))


def edge_forward_kernel(first, tile, slot, *refs):
    refs, (x_sel, slope), outs, (hidden, part) = (
        refs[: -NX - NZ - 4],
        refs[-NX - NZ - 4 : -NX - NZ - 2],
        refs[-NX - NZ - 2 : -2],
        refs[-2:],
    )
    *xs, x_early, slope_early, hidden_early, adj, w_in, bias = refs
    x_sel[...] = x_early[...]
    slope[...] = slope_early[...]
    hidden[...] = hidden_early[...]
    part[...] = jnp.zeros_like(part)
    edge_tiles(tile, first, xs, w_in, bias, x_sel, slope, hidden)

    def step(j, _):
        part[slot[j]] += jnp.dot(adj[j], hidden[j], preferred_element_type=F32)
        return 0

    lax.fori_loop(0, adj.shape[0], step, 0, unroll=4)
    for a in range(NX):
        outs[a][...] = part[a * NZ : (a + 1) * NZ, :, :HALF].astype(BF16)
    for r in range(NZ):
        for a in range(NX):
            outs[NX + r][a] = part[a * NZ + r, :, HALF:].astype(BF16)


def edge_forward(first, tile, slot, xs, early, adj, w_in, bias):
    count, rows, width = early[0].shape
    block = jax.ShapeDtypeStruct((count, rows, width), BF16)
    by_x = jax.ShapeDtypeStruct((NZ, rows, HALF), BF16)
    by_z = jax.ShapeDtypeStruct((NX, rows, width - HALF), BF16)
    return pl.pallas_call(
        lambda *refs: edge_forward_kernel(first, *refs),
        out_shape=(block, block) + (by_x,) * NX + (by_z,) * NZ,
        in_specs=[SMEM, SMEM] + [VMEM] * (len(xs) + 6),
        out_specs=(VMEM,) * (2 + NX + NZ),
        scratch_shapes=[
            pltpu.VMEM((count, rows, width), BF16),
            pltpu.VMEM((GRID_N, rows, width), F32),
        ],
        compiler_params=kernel_params(),
        name="edge_forward",
    )(tile, slot, *xs, *early, adj, w_in, bias.reshape(1, -1))


def times_transposed(a, b):
    return lax.dot_general(a, b, (((1,), (1,)), ((), ())), preferred_element_type=F32)


def transposed_times(a, b):
    return lax.dot_general(a, b, (((0,), (0,)), ((), ())), preferred_element_type=F32)


def node_kernel(
    agg_a, agg_b, mesh_lat, cot, w_out, w_node, gain, mesh_out, u_a, u_b, active_out, agg_out, d_agg_out
):
    agg = jnp.concatenate([agg_a[...], agg_b[...]], axis=1)
    high = agg.astype(BF16)
    low = (agg - high.astype(F32)).astype(BF16)
    aggregate = jnp.dot(high, w_out[...], preferred_element_type=F32) + jnp.dot(
        low, w_out[...], preferred_element_type=F32
    )
    summed = mesh_lat[...].astype(F32) + aggregate
    centred = summed - jnp.mean(summed, axis=-1, keepdims=True)
    inverse = lax.rsqrt(jnp.mean(centred * centred, axis=-1, keepdims=True) + EPSILON)
    standard = centred * inverse
    normed = standard * gain[...]
    gate = sigmoid(normed)
    active = (normed * gate).astype(BF16)
    mesh_out[...] = (summed + jnp.dot(active, w_node[...], preferred_element_type=F32)).astype(BF16)
    d_active = times_transposed(cot[...], w_node[...])
    d_standard = d_active * (gate * (1.0 + normed * (1.0 - gate))) * gain[...]
    first = jnp.mean(d_standard, axis=-1, keepdims=True)
    second = jnp.mean(d_standard * standard, axis=-1, keepdims=True)
    d_summed = cot[...].astype(F32) + inverse * (d_standard - first - standard * second)
    d_agg = d_summed.astype(BF16)
    u = times_transposed(d_agg, w_out[...]).astype(BF16)
    u_a[...] = u[:, :HALF]
    u_b[...] = u[:, HALF:]
    active_out[...] = active
    agg_out[...] = high
    d_agg_out[...] = d_agg


def node_step(agg_a, agg_b, mesh_lat, cot, w_out, w_node, gain):
    rows, width = mesh_lat.shape
    whole = jax.ShapeDtypeStruct((rows, width), BF16)
    return pl.pallas_call(
        node_kernel,
        out_shape=(
            whole,
            jax.ShapeDtypeStruct((rows, HALF), BF16),
            jax.ShapeDtypeStruct((rows, width - HALF), BF16),
            whole,
            whole,
            whole,
        ),
        in_specs=[VMEM] * 7,
        out_specs=(VMEM,) * 6,
        compiler_params=kernel_params(),
        name="node_step",
    )(agg_a, agg_b, mesh_lat, cot, w_out, w_node, gain.reshape(1, -1))


def edge_backward_kernel(slot, flipped, out_place, *refs):
    refs, outs, (u_first, u_second, back) = refs[: -MESH_N - 3], refs[-MESH_N - 3 : -3], refs[-3:]
    *refs, adj, slope, ids, d_pre = refs
    lay_out(u_first, refs[:-NZ])
    lay_out(u_second, refs[-NZ:])
    rows = slope.shape[1]

    def step(j, _):
        u = jnp.concatenate([u_first[slot[j]], u_second[flipped[j]]], axis=1)
        term = (transposed_times(adj[j], u) * slope[j].astype(F32)).astype(BF16)
        d_pre[j] = term
        back[out_place[j]] = term
        return 0

    lax.fori_loop(0, adj.shape[0], step, 0, unroll=4)
    for i, ref in enumerate(outs):
        for q in range(4):
            ref[q * rows : (q + 1) * rows] = back[4 * i + q]
        ref[4 * rows :] = ids[i]


def edge_backward(slot, flipped, out_place, u_a, u_b, adj, slope, ids):
    count, rows, width = slope.shape
    return pl.pallas_call(
        edge_backward_kernel,
        out_shape=(jax.ShapeDtypeStruct(slope.shape, BF16),)
        + (jax.ShapeDtypeStruct((4 * rows + ids.shape[1], width), BF16),) * MESH_N,
        in_specs=[SMEM] * 3 + [VMEM] * (len(u_a) + len(u_b) + 3),
        out_specs=(VMEM,) * (1 + MESH_N),
        scratch_shapes=[
            pltpu.VMEM((GRID_N, rows, HALF), BF16),
            pltpu.VMEM((GRID_N, rows, width - HALF), BF16),
            pltpu.VMEM((4 * MESH_N, rows, width), BF16),
        ],
        compiler_params=kernel_params(),
        name="edge_backward",
    )(slot, flipped, out_place, *u_a, *u_b, adj, slope, ids)


def row_kernel(place, *refs):
    parts = refs[:MESH_N]
    w_in, out, acc = refs[MESH_N:]
    acc[...] = jnp.zeros_like(acc)
    blocks, rows, width = acc.shape
    for s, ref in enumerate(parts):
        for q in range(4):
            index = place[s * 4 + q]

            @pl.when(index >= 0)
            def _():
                acc[index] += ref[q * rows : (q + 1) * rows].astype(F32)

    for i in range(0, blocks, 2):
        row_sum = acc[i : i + 2].reshape(2 * rows, width).astype(BF16)
        out[i * rows : (i + 2) * rows] = times_transposed(row_sum, w_in[...]).astype(BF16)


def row_step(parts, w_in, blocks, rows):
    width = w_in.shape[0]
    place = jnp.stack([p[4 * rows, :4] for p in parts]).astype(jnp.int32).reshape(-1)
    return pl.pallas_call(
        row_kernel,
        out_shape=jax.ShapeDtypeStruct((blocks * rows, width), BF16),
        in_specs=[SMEM] + [VMEM] * (MESH_N + 1),
        out_specs=VMEM,
        scratch_shapes=[pltpu.VMEM((blocks, rows, width), F32)],
        compiler_params=kernel_params(),
        name="row_step",
    )(place, *parts, w_in)


def pick(v, index):
    return lax.dynamic_index_in_dim(v, index, 0, keepdims=False)


def reduce_core(v, my_core):
    rows, width = v.shape
    v = v.reshape(NY, 2, rows // MESH_N, width)
    keep = lax.dynamic_index_in_dim(v, my_core, 1, keepdims=False)
    return total([keep, send_y(lax.dynamic_index_in_dim(v, 1 - my_core, 1, keepdims=False), 0, 1)])


def reduce_y(v, my_y):
    parts = [pick(v, (my_y + k) % NY) for k in range(NY)]
    return total([parts[0]] + [send_y(parts[k], k, 0) for k in (2, 1, 3)])


def reduce_grid(v):
    rows, width = v.shape
    v = lax.all_to_all(v.reshape(GRID_N, rows // GRID_N, width), "grid", 0, 0)
    return v.astype(F32).sum(0).astype(BF16)


def spread_grid(v):
    rows, width = v.shape
    v = lax.all_to_all(jnp.broadcast_to(v[None], (GRID_N, rows, width)), "grid", 0, 0)
    return v.reshape(GRID_N * rows, width)


def spread_y(v):
    return jnp.stack([v] + [send_y(v, -k, 0) for k in (1, 2, 3)])


def finish_kernel(scales, me, mine, other, *outs):
    run = mine.shape[1]
    width = outs[0].shape[1]
    for k in range(NY):
        y = lax.rem(me[0] + k, NY)
        for ref, core in ((mine, me[1]), (other, 1 - me[1])):
            rows = pl.ds(pl.multiple_of((2 * y + core) * run, run), run)
            for i, out in enumerate(outs):
                out[rows, :] = ref[k, :, i * width : (i + 1) * width].astype(F32) * scales[i]


def finish(me, mine, other, width, scales):
    return pl.pallas_call(
        lambda *refs: finish_kernel(scales, *refs),
        out_shape=(jax.ShapeDtypeStruct((width, width), F32),) * 3,
        in_specs=[SMEM, VMEM, VMEM],
        out_specs=(VMEM,) * 3,
        compiler_params=kernel_params(),
        name="finish",
    )(me, mine, other)


def shards(
    grid_lat,
    mesh_lat,
    edge_grid_block,
    edge_mesh_block,
    edge_sender,
    edge_receiver,
    edge_live,
    weight_in,
    bias_in,
    weight_out,
    norm_gain,
    weight_node,
    cotangent,
):
    block_rows, width = mesh_lat.shape
    local_blocks = grid_lat.shape[0] // block_rows
    edge_blocks = edge_grid_block.shape[0]
    slot_count = edge_sender.shape[0] // edge_blocks
    g, m = lax.axis_index("grid"), lax.axis_index("mesh")
    my_x, my_z, my_y, my_core = g // NZ, g % NZ, m // 2, m % 2

    holder, place = edge_grid_block // local_blocks, edge_grid_block % local_blocks
    rel_holder = ((holder // 2 - my_y) % NY) * 2 + ((holder % 2) ^ my_core)
    seat = jnp.where(rel_holder // 2 == 1, rel_holder + 2, rel_holder)
    seat = jnp.where(rel_holder // 2 == 2, rel_holder - 2, seat)
    tile = seat * local_blocks + place
    rel_x, rel_z = (edge_mesh_block // NZ - my_x) % NX, (edge_mesh_block % NZ - my_z) % NZ
    slot, flipped = rel_x * NZ + rel_z, rel_z * NX + rel_x
    earlier = jnp.arange(edge_blocks)[None, :] < jnp.arange(edge_blocks)[:, None]
    rank = jnp.sum((rel_holder[:, None] == rel_holder[None, :]) & earlier, axis=1).astype(jnp.int32)
    out_place = rel_holder * 4 + rank

    lane = jnp.arange(width, dtype=jnp.int32)
    goes = out_place[:, None, None] == jnp.arange(MESH_N, dtype=jnp.int32)[:, None] * 4 + lane
    goes = goes & (lane < 4)
    ids = jnp.sum(jnp.where(goes, place[:, None, None] + 1, 0), axis=0) - 1
    ids = jnp.broadcast_to(ids.astype(BF16)[:, None, :], (MESH_N, 16, width))

    sender = edge_sender.reshape(edge_blocks, slot_count)
    receiver = edge_receiver.reshape(edge_blocks, slot_count)
    lanes = jnp.arange(block_rows, dtype=jnp.int32)
    live = jnp.arange(slot_count, dtype=jnp.int32)[None, :] < edge_live[:, None]
    send_hot = (sender[:, :, None] == lanes).astype(BF16)
    receive_hot = ((receiver[:, :, None] == lanes) & live[:, :, None]).astype(BF16)
    adj = jnp.einsum("ker,ket->krt", receive_hot, send_hot, preferred_element_type=F32).astype(BF16)

    own = grid_lat.reshape(local_blocks, block_rows, width)
    low, high = own[: local_blocks // 2], own[local_blocks // 2 :]
    far = send_y(own, 2)
    near = [send_y(low, -1), send_y(low, 1), send_y(high, -1), send_y(high, 1)]
    early = [own, send_y(own, 0, 1), far, send_y(far, 0, 1)]
    early = edge_early(tile, early, weight_in, bias_in)
    cross = [send_y(v, 0, 1) for v in near[:2]]
    near[2], near[3], adj, slot, flipped, out_place, ids, *early = order_together(
        near[2], near[3], adj, slot, flipped, out_place, ids, *early
    )
    cross += [send_y(v, 0, 1) for v in near[2:]]
    first = 4 * local_blocks
    late = [near[0], near[2], cross[0], cross[2], near[1], near[3], cross[1], cross[3]]
    x_sel, slope, *parts = edge_forward(first, tile, slot, late, early, adj, weight_in, bias_in)

    z_sums = scatter_z_ring(parts[NX:])
    x_sums = scatter_x_twice(parts[:NX])
    agg_a = scatter_z_twice([x_sums[r] for r in range(NZ)], F32)
    agg_b = scatter_x([z_sums[r] for r in range(NX)], F32)

    mesh_out, u_a, u_b, active, agg, d_agg = node_step(
        agg_a, agg_b, mesh_lat, cotangent, weight_out, weight_node, norm_gain
    )
    u_b = jnp.stack([u_b] + [send_x(u_b, -k) for k in range(1, NX)])
    u_a = gather_z_twice(u_a).reshape(NZ, block_rows, HALF)
    u_a = gather_x_twice(u_a)
    u_b = gather_z_ring(u_b)

    d_pre, *back = edge_backward(slot, flipped, out_place, u_a, u_b, adj, slope, ids)

    in_term = transposed_times(
        x_sel.reshape(edge_blocks * block_rows, width), d_pre.reshape(edge_blocks * block_rows, width)
    )
    node_term, out_term = transposed_times(active, cotangent), transposed_times(agg, d_agg)
    sums = jnp.concatenate([in_term, out_term, node_term], axis=1).astype(BF16)

    got = [back[0]] + [None] * (MESH_N - 1)
    for k in (0, 2, 1, 3):
        for c in range(2):
            if k or c:
                got[((NY - k) % NY) * 2 + c] = send_y(back[k * 2 + c], k, c)
    sums = reduce_core(sums, my_core)
    sums, got[1] = order_together(sums, got[1])
    sums = reduce_y(sums, my_y)
    sums = reduce_grid(sums.reshape(-1, sums.shape[-1]))
    sums, got[4], got[5] = order_together(sums, got[4], got[5])
    sums = spread_grid(sums)
    sums, got[6], got[2] = order_together(sums, got[6], got[2])
    sums = spread_y(sums)
    sums, got[7], got[3] = order_together(sums, got[7], got[3])
    others = send_y(sums, 0, 1)

    grid_grad = row_step(got, weight_in, local_blocks, block_rows)

    by_edge = 1.0 / math.sqrt(edge_blocks * slot_count * GRID_N * MESH_N)
    by_node = 1.0 / math.sqrt(block_rows * GRID_N * MESH_N)
    me = jnp.stack([my_y, my_core]).astype(jnp.int32)
    grad_in, grad_out, grad_node = finish(me, sums, others, width, (by_edge, by_edge, by_node))
    return (mesh_out, grid_grad, grad_in, grad_out, grad_node)


def solution(mesh):
    rows = P(("grid", "mesh"), None)
    line = P(("grid", "mesh"))
    return jax.shard_map(
        shards,
        mesh=mesh,
        in_specs=(rows, rows, line, line, line, line, line, P(), P(), P(), P(), P(), rows),
        out_specs=(rows, rows, P(), P(), P()),
        check_vma=False,
    )
```

```python
import math

import jax
import jax.numpy as jnp
from jax import lax
from jax.experimental import pallas as pl
from jax.experimental.pallas import tpu as pltpu
from jax.sharding import PartitionSpec as P

EPSILON = 1e-05
F32, BF16 = jnp.float32, jnp.bfloat16
NX, NZ, NY = 4, 8, 4
GRID_N, MESH_N = NX * NZ, 2 * NY
HALF = 256
VMEM = pl.BlockSpec(memory_space=pltpu.VMEM)
SMEM = pl.BlockSpec(memory_space=pltpu.SMEM)


def sigmoid(v):
    return 0.5 + 0.5 * jnp.tanh(0.5 * v)


def kernel_params(mib):
    return pltpu.CompilerParams(vmem_limit_bytes=mib * 1024 * 1024)


def send_y(v, k, c):
    pairs = [(m, ((m // 2 + k) % NY) * 2 + ((m % 2) ^ c)) for m in range(MESH_N)]
    return lax.ppermute(v, "mesh", pairs)


def send_x(v, k):
    return lax.ppermute(v, "grid", [(g, ((g // NZ + k) % NX) * NZ + g % NZ) for g in range(GRID_N)])


def send_z(v, k):
    return lax.ppermute(v, "grid", [(g, (g // NZ) * NZ + (g % NZ + k) % NZ) for g in range(GRID_N)])


def order_together(*values):
    return lax.optimization_barrier(values)


def total(parts, dtype=BF16):
    t = parts[0].astype(F32)
    for p in parts[1:]:
        t = t + p.astype(F32)
    return t.astype(dtype)


def join(*parts):
    return jnp.concatenate(parts, axis=0)


def scatter_x(parts, dtype=BF16):
    return total([parts[0]] + [send_x(parts[k], k) for k in (2, 1, 3)], dtype)


def scatter_x_twice(parts):
    h = parts[2].shape[0] // 2
    up, down = send_x(parts[2][:h], 1), send_x(parts[2][h:], -1)
    up = send_x(join(total([up, parts[1][:h]]), parts[1][h:]), 1)
    down = send_x(join(parts[3][:h], total([down, parts[3][h:]])), -1)
    return total([parts[0], up, down])


def scatter_z_twice(parts, dtype=BF16):
    n = parts[0].shape[0]
    far = send_z(parts[4], 4)
    up = send_z(join(parts[2], parts[3]), 2)
    down = send_z(join(parts[6], parts[5]), -2)
    up_one = send_z(total([parts[1], up[n:]]), 1)
    down_one = send_z(total([parts[7], down[n:]]), -1)
    return total([parts[0], far, up[:n], down[:n], up_one, down_one], dtype)


def gather_z_twice(v):
    n = v.shape[0]
    up, down = send_z(v, 1), send_z(v, -1)
    late, up, down = order_together(v, up, down)
    far = send_z(late, 4)
    up_two, down_two = send_z(join(v, up), 2), send_z(join(v, down), -2)
    return join(v, down, down_two, far, up_two[n:], up_two[:n], up)


def gather_x_twice(v):
    h = v.shape[0] // 2
    up, down = send_x(v, 1), send_x(v, -1)
    return [v, down, send_x(down[:h], -1), send_x(up[h:], 1), up]


def scatter_z_ring(parts):
    up, down = send_z(parts[3], 1), send_z(parts[4], -1)
    up, down = total([up, parts[2]]), total([down, parts[5]])
    up, down = send_z(up, 1), send_z(down, -1)
    up, down = total([up, parts[1]]), total([down, parts[6]])
    up, down = send_z(up, 1), send_z(down, -1)
    down = send_z(total([down, parts[7]]), -1)
    return total([parts[0], up, down])


def gather_z_ring(v):
    out = [v] + [None] * (NZ - 1)
    up = down = v
    for k in range(1, 5):
        if k < 4:
            up = send_z(up, 1)
            out[NZ - k] = up
        down = send_z(down, -1)
        out[k] = down
    return out


def select_tile(index, arrays, write):
    start = 0
    for ref in arrays:
        lo, hi = start, start + ref.shape[0]

        @pl.when((index >= lo) & (index < hi))
        def _():
            write(ref, index - lo)

        start = hi


def edge_forward_kernel(tile, slot, fresh, touched, *refs):
    xs = refs[:MESH_N]
    adj, w_in, bias = refs[MESH_N : MESH_N + 3]
    x_sel, slope = refs[MESH_N + 3 : MESH_N + 5]
    outs = refs[MESH_N + 5 : -1]
    part = refs[-1]
    count = adj.shape[0]

    def step(i, _):
        for r in range(2):
            j = 2 * i + r

            def write(ref, place):
                x_sel[j] = ref[place]

            select_tile(tile[j], xs, write)
        rows = x_sel[pl.ds(2 * i, 2)]
        rows = rows.reshape(2 * rows.shape[1], rows.shape[2])
        pre = jnp.dot(rows, w_in[...], preferred_element_type=F32) + bias[...]
        gate = sigmoid(pre)
        hidden = (pre * gate).astype(BF16)
        rise = (gate * (1.0 + pre * (1.0 - gate))).astype(BF16)
        for r in range(2):
            j = 2 * i + r
            slope[j] = rise[r * 128 : (r + 1) * 128]
            term = jnp.dot(adj[j], hidden[r * 128 : (r + 1) * 128], preferred_element_type=F32)

            @pl.when(fresh[j] == 1)
            def _():
                part[slot[j]] = term

            @pl.when(fresh[j] == 0)
            def _():
                part[slot[j]] += term

        return 0

    lax.fori_loop(0, count // 2, step, 0, unroll=2)
    for a in range(NX):
        for r in range(NZ):
            i = a * NZ + r

            @pl.when(touched[i] == 1)
            def _():
                outs[a][r] = part[i, :, :HALF].astype(BF16)
                outs[NX + r][a] = part[i, :, HALF:].astype(BF16)

            @pl.when(touched[i] == 0)
            def _():
                outs[a][r] = jnp.zeros(outs[a].shape[1:], BF16)
                outs[NX + r][a] = jnp.zeros(outs[NX + r].shape[1:], BF16)


def edge_forward(tile, slot, fresh, touched, xs, adj, w_in, bias):
    count, rows, width = adj.shape[0], xs[0].shape[1], xs[0].shape[2]
    block = jax.ShapeDtypeStruct((count, rows, width), BF16)
    by_x = jax.ShapeDtypeStruct((NZ, rows, HALF), BF16)
    by_z = jax.ShapeDtypeStruct((NX, rows, width - HALF), BF16)
    return pl.pallas_call(
        edge_forward_kernel,
        out_shape=(block, block) + (by_x,) * NX + (by_z,) * NZ,
        in_specs=[SMEM] * 4 + [VMEM] * (MESH_N + 3),
        out_specs=(VMEM,) * (2 + NX + NZ),
        scratch_shapes=[pltpu.VMEM((GRID_N, rows, width), F32)],
        compiler_params=kernel_params(32),
        name="edge_forward",
    )(tile, slot, fresh, touched, *xs, adj, w_in, bias.reshape(1, -1))


def times_transposed(a, b):
    return lax.dot_general(a, b, (((1,), (1,)), ((), ())), preferred_element_type=F32)


def transposed_times(a, b):
    return lax.dot_general(a, b, (((0,), (0,)), ((), ())), preferred_element_type=F32)


def node_kernel(
    agg_a, agg_b, mesh_lat, cot, w_out, w_node, gain, mesh_out, u_a, u_b, active_out, agg_out, d_agg_out
):
    agg = jnp.concatenate([agg_a[...], agg_b[...]], axis=1)
    high = agg.astype(BF16)
    low = (agg - high.astype(F32)).astype(BF16)
    aggregate = jnp.dot(high, w_out[...], preferred_element_type=F32) + jnp.dot(
        low, w_out[...], preferred_element_type=F32
    )
    summed = mesh_lat[...].astype(F32) + aggregate
    centred = summed - jnp.mean(summed, axis=-1, keepdims=True)
    inverse = lax.rsqrt(jnp.mean(centred * centred, axis=-1, keepdims=True) + EPSILON)
    standard = centred * inverse
    normed = standard * gain[...]
    gate = sigmoid(normed)
    active = (normed * gate).astype(BF16)
    mesh_out[...] = (summed + jnp.dot(active, w_node[...], preferred_element_type=F32)).astype(BF16)
    d_active = times_transposed(cot[...], w_node[...])
    d_standard = d_active * (gate * (1.0 + normed * (1.0 - gate))) * gain[...]
    first = jnp.mean(d_standard, axis=-1, keepdims=True)
    second = jnp.mean(d_standard * standard, axis=-1, keepdims=True)
    d_summed = cot[...].astype(F32) + inverse * (d_standard - first - standard * second)
    d_agg = d_summed.astype(BF16)
    u = times_transposed(d_agg, w_out[...]).astype(BF16)
    u_a[...] = u[:, :HALF]
    u_b[...] = u[:, HALF:]
    active_out[...] = active
    agg_out[...] = high
    d_agg_out[...] = d_agg


def node_step(agg_a, agg_b, mesh_lat, cot, w_out, w_node, gain):
    rows, width = mesh_lat.shape
    whole = jax.ShapeDtypeStruct((rows, width), BF16)
    return pl.pallas_call(
        node_kernel,
        out_shape=(
            whole,
            jax.ShapeDtypeStruct((rows, HALF), BF16),
            jax.ShapeDtypeStruct((rows, width - HALF), BF16),
            whole,
            whole,
            whole,
        ),
        in_specs=[VMEM] * 7,
        out_specs=(VMEM,) * 6,
        compiler_params=kernel_params(12),
        name="node_step",
    )(agg_a, agg_b, mesh_lat, cot, w_out, w_node, gain.reshape(1, -1))


def edge_backward_kernel(slot, flipped, out_place, *refs):
    refs, outs, (u_first, u_second, back) = refs[: -MESH_N - 3], refs[-MESH_N - 3 : -3], refs[-3:]
    *refs, adj, slope, d_pre = refs
    for scratch, pieces in ((u_first, refs[:-NZ]), (u_second, refs[-NZ:])):
        start = 0
        for ref in pieces:
            scratch[start : start + ref.shape[0]] = ref[...]
            start += ref.shape[0]

    def step(j, _):
        u = jnp.concatenate([u_first[slot[j]], u_second[flipped[j]]], axis=1)
        term = (transposed_times(adj[j], u) * slope[j].astype(F32)).astype(BF16)
        d_pre[j] = term
        back[out_place[j]] = term
        return 0

    lax.fori_loop(0, adj.shape[0], step, 0, unroll=4)
    for i, ref in enumerate(outs):
        ref[...] = back[4 * i : 4 * (i + 1)]


def edge_backward(slot, flipped, out_place, u_a, u_b, adj, slope):
    count, rows, width = slope.shape
    return pl.pallas_call(
        edge_backward_kernel,
        out_shape=(jax.ShapeDtypeStruct(slope.shape, BF16),)
        + (jax.ShapeDtypeStruct((4, rows, width), BF16),) * MESH_N,
        in_specs=[SMEM] * 3 + [VMEM] * (len(u_a) + len(u_b) + 2),
        out_specs=(VMEM,) * (1 + MESH_N),
        scratch_shapes=[
            pltpu.VMEM((GRID_N, rows, HALF), BF16),
            pltpu.VMEM((GRID_N, rows, width - HALF), BF16),
            pltpu.VMEM((4 * MESH_N, rows, width), BF16),
        ],
        compiler_params=kernel_params(26),
        name="edge_backward",
    )(slot, flipped, out_place, *u_a, *u_b, adj, slope)


def row_kernel(place, *refs):
    parts = refs[:MESH_N]
    w_in, out, acc = refs[MESH_N:]
    acc[...] = jnp.zeros_like(acc)
    for s, ref in enumerate(parts):
        for q in range(4):

            @pl.when(place[s * 4 + q] >= 0)
            def _():
                acc[place[s * 4 + q]] += ref[q].astype(F32)

    blocks, rows, width = acc.shape
    for i in range(0, blocks, 2):
        row_sum = acc[i : i + 2].reshape(2 * rows, width).astype(BF16)
        out[i * rows : (i + 2) * rows] = times_transposed(row_sum, w_in[...]).astype(BF16)


def row_step(place, parts, w_in, blocks):
    _, rows, width = parts[0].shape
    return pl.pallas_call(
        row_kernel,
        out_shape=jax.ShapeDtypeStruct((blocks * rows, width), BF16),
        in_specs=[SMEM] + [VMEM] * (MESH_N + 1),
        out_specs=VMEM,
        scratch_shapes=[pltpu.VMEM((blocks, rows, width), F32)],
        compiler_params=kernel_params(16),
        name="row_step",
    )(place, *parts, w_in)


def pick(v, index):
    return lax.dynamic_index_in_dim(v, index, 0, keepdims=False)


def reduce_core(v, my_core):
    rows, width = v.shape
    v = v.reshape(NY, 2, rows // MESH_N, width)
    keep = lax.dynamic_index_in_dim(v, my_core, 1, keepdims=False)
    return total([keep, send_y(lax.dynamic_index_in_dim(v, 1 - my_core, 1, keepdims=False), 0, 1)])


def reduce_y(v, my_y):
    parts = [pick(v, (my_y + k) % NY) for k in range(NY)]
    return total([parts[0]] + [send_y(parts[k], k, 0) for k in (2, 1, 3)])


def reduce_grid(v):
    rows, width = v.shape
    v = lax.all_to_all(v.reshape(GRID_N, rows // GRID_N, width), "grid", 0, 0)
    return v.astype(F32).sum(0).astype(BF16)


def spread_grid(v):
    rows, width = v.shape
    v = lax.all_to_all(jnp.broadcast_to(v[None], (GRID_N, rows, width)), "grid", 0, 0)
    return v.reshape(GRID_N * rows, width)


def spread_y(v):
    return jnp.stack([v] + [send_y(v, -k, 0) for k in (1, 2, 3)])


def finish_kernel(scales, me, mine, other, *outs):
    run = mine.shape[1]
    width = outs[0].shape[1]
    for k in range(NY):
        y = lax.rem(me[0] + k, NY)
        for ref, core in ((mine, me[1]), (other, 1 - me[1])):
            rows = pl.ds(pl.multiple_of((2 * y + core) * run, run), run)
            for i, out in enumerate(outs):
                out[rows, :] = ref[k, :, i * width : (i + 1) * width].astype(F32) * scales[i]


def finish(me, mine, other, width, scales):
    return pl.pallas_call(
        lambda *refs: finish_kernel(scales, *refs),
        out_shape=(jax.ShapeDtypeStruct((width, width), F32),) * 3,
        in_specs=[SMEM, VMEM, VMEM],
        out_specs=(VMEM,) * 3,
        compiler_params=kernel_params(12),
        name="finish",
    )(me, mine, other)


def shards(
    grid_lat,
    mesh_lat,
    edge_grid_block,
    edge_mesh_block,
    edge_sender,
    edge_receiver,
    edge_live,
    weight_in,
    bias_in,
    weight_out,
    norm_gain,
    weight_node,
    cotangent,
):
    block_rows, width = mesh_lat.shape
    local_blocks = grid_lat.shape[0] // block_rows
    edge_blocks = edge_grid_block.shape[0]
    slot_count = edge_sender.shape[0] // edge_blocks
    g, m = lax.axis_index("grid"), lax.axis_index("mesh")
    my_x, my_z, my_y, my_core = g // NZ, g % NZ, m // 2, m % 2

    holder, place = edge_grid_block // local_blocks, edge_grid_block % local_blocks
    rel_holder = ((holder // 2 - my_y) % NY) * 2 + ((holder % 2) ^ my_core)
    tile = rel_holder * local_blocks + place
    rel_x, rel_z = (edge_mesh_block // NZ - my_x) % NX, (edge_mesh_block % NZ - my_z) % NZ
    slot, flipped = rel_x * NZ + rel_z, rel_z * NX + rel_x
    earlier = jnp.arange(edge_blocks)[None, :] < jnp.arange(edge_blocks)[:, None]
    rank = jnp.sum((rel_holder[:, None] == rel_holder[None, :]) & earlier, axis=1).astype(jnp.int32)
    out_place = rel_holder * 4 + rank
    fresh = 1 - jnp.any((slot[:, None] == slot[None, :]) & earlier, axis=1).astype(jnp.int32)
    owners = jnp.arange(GRID_N, dtype=jnp.int32)
    touched = jnp.any(slot[:, None] == owners[None, :], axis=0).astype(jnp.int32)

    own = grid_lat.reshape(local_blocks, block_rows, width)
    same = [own] + [None] * 3
    for k in (2, 1, 3):
        same[k] = send_y(own, -k, 0)
    other_own = send_y(own, 0, 1)

    table = jnp.stack([edge_grid_block] + [send_y(edge_grid_block, -k, 0) for k in (1, 2, 3)])
    table = jnp.stack([table, send_y(table, 0, 1)], axis=1).reshape(MESH_N, edge_blocks)
    mine = (table // local_blocks == m)[:, :, None]
    order = jnp.cumsum(mine.astype(jnp.int32), axis=1) - 1
    hit = mine & (order == jnp.arange(4, dtype=jnp.int32))
    returned = jnp.sum(jnp.where(hit, (table % local_blocks)[:, :, None] + 1, 0), axis=1) - 1
    returned = returned.reshape(-1)

    sender = edge_sender.reshape(edge_blocks, slot_count)
    receiver = edge_receiver.reshape(edge_blocks, slot_count)
    lanes = jnp.arange(block_rows, dtype=jnp.int32)
    live = jnp.arange(slot_count, dtype=jnp.int32)[None, :] < edge_live[:, None]
    send_hot = (sender[:, :, None] == lanes).astype(BF16)
    receive_hot = ((receiver[:, :, None] == lanes) & live[:, :, None]).astype(BF16)
    adj = jnp.einsum("ker,ket->krt", receive_hot, send_hot, preferred_element_type=F32).astype(BF16)

    same[1], adj, tile, slot, flipped, out_place, fresh, touched, returned = order_together(
        same[1], adj, tile, slot, flipped, out_place, fresh, touched, returned
    )
    other = [other_own] + [send_y(v, 0, 1) for v in same[1:]]
    xs = [v for pair in zip(same, other) for v in pair]

    x_sel, slope, *parts = edge_forward(tile, slot, fresh, touched, xs, adj, weight_in, bias_in)

    z_sums = scatter_z_ring(parts[NX:])
    x_sums = scatter_x_twice(parts[:NX])
    agg_a = scatter_z_twice([x_sums[r] for r in range(NZ)], F32)
    agg_b = scatter_x([z_sums[r] for r in range(NX)], F32)

    mesh_out, u_a, u_b, active, agg, d_agg = node_step(
        agg_a, agg_b, mesh_lat, cotangent, weight_out, weight_node, norm_gain
    )
    u_b = jnp.stack([u_b] + [send_x(u_b, -k) for k in range(1, NX)])
    u_a = gather_z_twice(u_a).reshape(NZ, block_rows, HALF)
    u_a = gather_x_twice(u_a)
    u_b = gather_z_ring(u_b)

    node_term, out_term = transposed_times(active, cotangent), transposed_times(agg, d_agg)
    early = jnp.concatenate([out_term, node_term], axis=1).astype(BF16)
    early = reduce_core(early, my_core)
    slope, early = order_together(slope, early)
    early = reduce_y(early, my_y)

    d_pre, *back = edge_backward(slot, flipped, out_place, u_a, u_b, adj, slope)

    in_term = transposed_times(
        x_sel.reshape(edge_blocks * block_rows, width), d_pre.reshape(edge_blocks * block_rows, width)
    )
    sums = in_term.astype(BF16)

    got = [back[0]] + [None] * (MESH_N - 1)
    for k in (0, 2, 1, 3):
        for c in range(2):
            if k or c:
                got[((NY - k) % NY) * 2 + c] = send_y(back[k * 2 + c], k, c)
    sums = reduce_core(sums, my_core)
    sums, got[1], early = order_together(sums, got[1], early)
    sums = jnp.concatenate([reduce_y(sums, my_y), early], axis=1)
    sums, got[4] = order_together(sums, got[4])
    sums = reduce_grid(sums.reshape(-1, sums.shape[-1]))
    sums, got[5] = order_together(sums, got[5])
    sums = spread_grid(sums)
    sums, got[6], got[2] = order_together(sums, got[6], got[2])
    sums = spread_y(sums)
    sums, got[7], got[3] = order_together(sums, got[7], got[3])
    others = send_y(sums, 0, 1)

    grid_grad = row_step(returned, got, weight_in, local_blocks)

    by_edge = 1.0 / math.sqrt(edge_blocks * slot_count * GRID_N * MESH_N)
    by_node = 1.0 / math.sqrt(block_rows * GRID_N * MESH_N)
    me = jnp.stack([my_y, my_core]).astype(jnp.int32)
    grad_in, grad_out, grad_node = finish(me, sums, others, width, (by_edge, by_edge, by_node))
    return (mesh_out, grid_grad, grad_in, grad_out, grad_node)


def solution(mesh):
    rows = P(("grid", "mesh"), None)
    line = P(("grid", "mesh"))
    return jax.shard_map(
        shards,
        mesh=mesh,
        in_specs=(rows, rows, line, line, line, line, line, P(), P(), P(), P(), P(), rows),
        out_specs=(rows, rows, P(), P(), P()),
        check_vma=False,
    )
```

```python
import math

import jax
import jax.numpy as jnp
from jax import lax
from jax.experimental import pallas as pl
from jax.experimental.pallas import tpu as pltpu
from jax.sharding import PartitionSpec as P

EPSILON = 1e-05
F32, BF16 = jnp.float32, jnp.bfloat16
NX, NZ, NY = 4, 8, 4
GRID_N, MESH_N = NX * NZ, 2 * NY
HALF = 256
VMEM = pl.BlockSpec(memory_space=pltpu.VMEM)
SMEM = pl.BlockSpec(memory_space=pltpu.SMEM)


def sigmoid(v):
    return 0.5 + 0.5 * jnp.tanh(0.5 * v)


def kernel_params():
    return pltpu.CompilerParams(vmem_limit_bytes=40 * 1024 * 1024)


def send_y(v, k, c=0):
    pairs = [(m, ((m // 2 + k) % NY) * 2 + ((m % 2) ^ c)) for m in range(MESH_N)]
    return lax.ppermute(v, "mesh", pairs)


def send_x(v, k):
    return lax.ppermute(v, "grid", [(g, ((g // NZ + k) % NX) * NZ + g % NZ) for g in range(GRID_N)])


def send_z(v, k):
    return lax.ppermute(v, "grid", [(g, (g // NZ) * NZ + (g % NZ + k) % NZ) for g in range(GRID_N)])


def order_together(*values):
    return lax.optimization_barrier(values)


def total(parts, dtype=BF16):
    t = parts[0].astype(F32)
    for p in parts[1:]:
        t = t + p.astype(F32)
    return t.astype(dtype)


def join(*parts):
    return jnp.concatenate(parts, axis=0)


def scatter_x(parts, dtype=BF16):
    return total([parts[0]] + [send_x(parts[k], k) for k in (1, 3, 2)], dtype)


def scatter_x_twice(parts):
    h = parts[2].shape[0] // 2
    up, down = send_x(parts[2][:h], 1), send_x(parts[2][h:], -1)
    up = send_x(join(total([up, parts[1][:h]]), parts[1][h:]), 1)
    down = send_x(join(parts[3][:h], total([down, parts[3][h:]])), -1)
    return total([parts[0], up, down])


def exchange_z(v):
    rows = [[x * NZ + z for z in range(NZ)] for x in range(NX)]
    return lax.all_to_all(v, "grid", 0, 0, axis_index_groups=rows)


def gather_x_twice(v):
    h = v.shape[0] // 2
    up, down = send_x(v, 1), send_x(v, -1)
    return [v, down, send_x(down[:h], -1), send_x(up[h:], 1), up]


def scatter_z_ring(parts):
    up, down = send_z(parts[3], 1), send_z(parts[4], -1)
    up, down = total([up, parts[2]]), total([down, parts[5]])
    up, down = send_z(up, 1), send_z(down, -1)
    up, down = total([up, parts[1]]), total([down, parts[6]])
    up, down = send_z(up, 1), send_z(down, -1)
    down = send_z(total([down, parts[7]]), -1)
    return total([parts[0], up, down])


def gather_z_ring(v):
    out = [v] + [None] * (NZ - 1)
    up = down = v
    for k in range(1, 5):
        if k < 4:
            up = send_z(up, 1)
            out[NZ - k] = up
        down = send_z(down, -1)
        out[k] = down
    return out


def select_tile(index, arrays, write):
    start = 0
    for ref in arrays:
        lo, hi = start, start + ref.shape[0]

        @pl.when((index >= lo) & (index < hi))
        def _():
            write(ref, index - lo)

        start = hi


def edge_forward_kernel(me, tile, slot, *refs):
    refs, outs, part = refs[: -NX - NZ - 1], refs[-NX - NZ - 1 : -1], refs[-1]
    *xs, adj, w_in, bias, x_sel, slope = refs
    part[...] = jnp.zeros_like(part)
    count = adj.shape[0]

    def step(i, _):
        for r in range(2):
            j = 2 * i + r

            def write(ref, place):
                x_sel[j] = ref[place]

            select_tile(tile[j], xs, write)
        rows = x_sel[pl.ds(2 * i, 2)]
        rows = rows.reshape(2 * rows.shape[1], rows.shape[2])
        pre = jnp.dot(rows, w_in[...], preferred_element_type=F32) + bias[...]
        gate = sigmoid(pre)
        hidden = (pre * gate).astype(BF16)
        rise = (gate * (1.0 + pre * (1.0 - gate))).astype(BF16)
        for r in range(2):
            j = 2 * i + r
            slope[j] = rise[r * 128 : (r + 1) * 128]
            term = jnp.dot(adj[j], hidden[r * 128 : (r + 1) * 128], preferred_element_type=F32)
            part[slot[j]] += term
        return 0

    lax.fori_loop(0, count // 2, step, 0, unroll=2)
    for a in range(NX):
        outs[a][...] = part[a * NZ : (a + 1) * NZ, :, :HALF].astype(BF16)
    for r in range(NZ):
        for a in range(NX):
            outs[NX + r][a] = part[a * NZ + lax.rem(me[0] + r, NZ), :, HALF:].astype(BF16)


def edge_forward(me, tile, slot, xs, adj, w_in, bias):
    count, rows, width = adj.shape[0], xs[0].shape[1], xs[0].shape[2]
    block = jax.ShapeDtypeStruct((count, rows, width), BF16)
    by_x = jax.ShapeDtypeStruct((NZ, rows, HALF), BF16)
    by_z = jax.ShapeDtypeStruct((NX, rows, width - HALF), BF16)
    return pl.pallas_call(
        edge_forward_kernel,
        out_shape=(block, block) + (by_x,) * NX + (by_z,) * NZ,
        in_specs=[SMEM] * 3 + [VMEM] * (len(xs) + 3),
        out_specs=(VMEM,) * (2 + NX + NZ),
        scratch_shapes=[pltpu.VMEM((GRID_N, rows, width), F32)],
        compiler_params=kernel_params(),
        name="edge_forward",
    )(me, tile, slot, *xs, adj, w_in, bias.reshape(1, -1))


def times_transposed(a, b):
    return lax.dot_general(a, b, (((1,), (1,)), ((), ())), preferred_element_type=F32)


def transposed_times(a, b):
    return lax.dot_general(a, b, (((0,), (0,)), ((), ())), preferred_element_type=F32)


def node_kernel(
    agg_a, agg_b, mesh_lat, cot, w_out, w_node, gain, mesh_out, u_a, u_b, active_out, agg_out, d_agg_out
):
    agg = jnp.concatenate([agg_a[...], agg_b[...]], axis=1)
    high = agg.astype(BF16)
    low = (agg - high.astype(F32)).astype(BF16)
    aggregate = jnp.dot(high, w_out[...], preferred_element_type=F32) + jnp.dot(
        low, w_out[...], preferred_element_type=F32
    )
    summed = mesh_lat[...].astype(F32) + aggregate
    centred = summed - jnp.mean(summed, axis=-1, keepdims=True)
    inverse = lax.rsqrt(jnp.mean(centred * centred, axis=-1, keepdims=True) + EPSILON)
    standard = centred * inverse
    normed = standard * gain[...]
    gate = sigmoid(normed)
    active = (normed * gate).astype(BF16)
    mesh_out[...] = (summed + jnp.dot(active, w_node[...], preferred_element_type=F32)).astype(BF16)
    d_active = times_transposed(cot[...], w_node[...])
    d_standard = d_active * (gate * (1.0 + normed * (1.0 - gate))) * gain[...]
    first = jnp.mean(d_standard, axis=-1, keepdims=True)
    second = jnp.mean(d_standard * standard, axis=-1, keepdims=True)
    d_summed = cot[...].astype(F32) + inverse * (d_standard - first - standard * second)
    d_agg = d_summed.astype(BF16)
    u = times_transposed(d_agg, w_out[...]).astype(BF16)
    u_a[...] = u[:, :HALF]
    u_b[...] = u[:, HALF:]
    active_out[...] = active
    agg_out[...] = high
    d_agg_out[...] = d_agg


def node_step(agg_a, agg_b, mesh_lat, cot, w_out, w_node, gain):
    rows, width = mesh_lat.shape
    whole = jax.ShapeDtypeStruct((rows, width), BF16)
    return pl.pallas_call(
        node_kernel,
        out_shape=(
            whole,
            jax.ShapeDtypeStruct((rows, HALF), BF16),
            jax.ShapeDtypeStruct((rows, width - HALF), BF16),
            whole,
            whole,
            whole,
        ),
        in_specs=[VMEM] * 7,
        out_specs=(VMEM,) * 6,
        compiler_params=kernel_params(),
        name="node_step",
    )(agg_a, agg_b, mesh_lat, cot, w_out, w_node, gain.reshape(1, -1))


def edge_backward_kernel(slot, flipped, out_place, *refs):
    refs, outs, (u_first, u_second, back) = refs[: -MESH_N - 3], refs[-MESH_N - 3 : -3], refs[-3:]
    *refs, adj, slope, d_pre = refs
    for scratch, pieces in ((u_first, refs[:-NZ]), (u_second, refs[-NZ:])):
        start = 0
        for ref in pieces:
            scratch[start : start + ref.shape[0]] = ref[...]
            start += ref.shape[0]

    def step(j, _):
        u = jnp.concatenate([u_first[slot[j]], u_second[flipped[j]]], axis=1)
        term = (transposed_times(adj[j], u) * slope[j].astype(F32)).astype(BF16)
        d_pre[j] = term
        back[out_place[j]] = term
        return 0

    lax.fori_loop(0, adj.shape[0], step, 0, unroll=4)
    for i, ref in enumerate(outs):
        ref[...] = back[4 * i : 4 * (i + 1)]


def edge_backward(slot, flipped, out_place, u_a, u_b, adj, slope):
    count, rows, width = slope.shape
    return pl.pallas_call(
        edge_backward_kernel,
        out_shape=(jax.ShapeDtypeStruct(slope.shape, BF16),)
        + (jax.ShapeDtypeStruct((4, rows, width), BF16),) * MESH_N,
        in_specs=[SMEM] * 3 + [VMEM] * (len(u_a) + len(u_b) + 2),
        out_specs=(VMEM,) * (1 + MESH_N),
        scratch_shapes=[
            pltpu.VMEM((GRID_N, rows, HALF), BF16),
            pltpu.VMEM((GRID_N, rows, width - HALF), BF16),
            pltpu.VMEM((4 * MESH_N, rows, width), BF16),
        ],
        compiler_params=kernel_params(),
        name="edge_backward",
    )(slot, flipped, out_place, *u_a, *u_b, adj, slope)


def row_kernel(place, *refs):
    parts = refs[:MESH_N]
    w_in, out, acc = refs[MESH_N:]
    acc[...] = jnp.zeros_like(acc)
    for s, ref in enumerate(parts):
        for q in range(4):

            @pl.when(place[s * 4 + q] >= 0)
            def _():
                acc[place[s * 4 + q]] += ref[q].astype(F32)

    blocks, rows, width = acc.shape
    for i in range(0, blocks, 2):
        row_sum = acc[i : i + 2].reshape(2 * rows, width).astype(BF16)
        out[i * rows : (i + 2) * rows] = times_transposed(row_sum, w_in[...]).astype(BF16)


def row_step(place, parts, w_in, blocks):
    _, rows, width = parts[0].shape
    return pl.pallas_call(
        row_kernel,
        out_shape=jax.ShapeDtypeStruct((blocks * rows, width), BF16),
        in_specs=[SMEM] + [VMEM] * (MESH_N + 1),
        out_specs=VMEM,
        scratch_shapes=[pltpu.VMEM((blocks, rows, width), F32)],
        compiler_params=kernel_params(),
        name="row_step",
    )(place, *parts, w_in)


def pick(v, index):
    return lax.dynamic_index_in_dim(v, index, 0, keepdims=False)


def reduce_core(v, my_core):
    rows, width = v.shape
    v = v.reshape(NY, 2, rows // MESH_N, width)
    keep = lax.dynamic_index_in_dim(v, my_core, 1, keepdims=False)
    return total([keep, send_y(lax.dynamic_index_in_dim(v, 1 - my_core, 1, keepdims=False), 0, 1)])


def reduce_y(v, my_y):
    parts = [pick(v, (my_y + k) % NY) for k in range(NY)]
    return total([parts[0]] + [send_y(parts[k], k, 0) for k in (2, 1, 3)])


def reduce_grid(v):
    rows, width = v.shape
    v = lax.all_to_all(v.reshape(GRID_N, rows // GRID_N, width), "grid", 0, 0)
    return v.astype(F32).sum(0).astype(BF16)


def spread_grid(v):
    rows, width = v.shape
    v = lax.all_to_all(jnp.broadcast_to(v[None], (GRID_N, rows, width)), "grid", 0, 0)
    return v.reshape(GRID_N * rows, width)


def spread_y(v):
    return jnp.stack([v] + [send_y(v, -k, 0) for k in (1, 2, 3)])


def finish_kernel(scales, me, mine, other, *outs):
    run = mine.shape[1]
    width = outs[0].shape[1]
    for k in range(NY):
        y = lax.rem(me[0] + k, NY)
        for ref, core in ((mine, me[1]), (other, 1 - me[1])):
            rows = pl.ds(pl.multiple_of((2 * y + core) * run, run), run)
            for i, out in enumerate(outs):
                out[rows, :] = ref[k, :, i * width : (i + 1) * width].astype(F32) * scales[i]


def finish(me, mine, other, width, scales):
    return pl.pallas_call(
        lambda *refs: finish_kernel(scales, *refs),
        out_shape=(jax.ShapeDtypeStruct((width, width), F32),) * 3,
        in_specs=[SMEM, VMEM, VMEM],
        out_specs=(VMEM,) * 3,
        compiler_params=kernel_params(),
        name="finish",
    )(me, mine, other)


def shards(
    grid_lat,
    mesh_lat,
    edge_grid_block,
    edge_mesh_block,
    edge_sender,
    edge_receiver,
    edge_live,
    weight_in,
    bias_in,
    weight_out,
    norm_gain,
    weight_node,
    cotangent,
):
    block_rows, width = mesh_lat.shape
    local_blocks = grid_lat.shape[0] // block_rows
    edge_blocks = edge_grid_block.shape[0]
    slot_count = edge_sender.shape[0] // edge_blocks
    g, m = lax.axis_index("grid"), lax.axis_index("mesh")
    my_x, my_z, my_y, my_core = g // NZ, g % NZ, m // 2, m % 2

    holder, place = edge_grid_block // local_blocks, edge_grid_block % local_blocks
    rel_holder = ((holder // 2 - my_y) % NY) * 2 + ((holder % 2) ^ my_core)
    tile = rel_holder * local_blocks + place
    rel_x, rel_z = (edge_mesh_block // NZ - my_x) % NX, (edge_mesh_block % NZ - my_z) % NZ
    slot, flipped = rel_x * NZ + edge_mesh_block % NZ, rel_z * NX + rel_x
    earlier = jnp.arange(edge_blocks)[None, :] < jnp.arange(edge_blocks)[:, None]
    rank = jnp.sum((rel_holder[:, None] == rel_holder[None, :]) & earlier, axis=1).astype(jnp.int32)
    out_place = rel_holder * 4 + rank

    own = grid_lat.reshape(local_blocks, block_rows, width)
    half = local_blocks // 2
    after, before = send_y(own, -1), send_y(own, 1)
    far = [send_y(before[:half], 1), send_y(after[half:], -1)]
    other_own, blocks = order_together(send_y(own, 0, 1), edge_grid_block)

    table = jnp.stack([blocks] + [send_y(blocks, -k, 0) for k in (1, 2, 3)])
    table = jnp.stack([table, send_y(table, 0, 1)], axis=1).reshape(MESH_N, edge_blocks)
    mine = (table // local_blocks == m)[:, :, None]
    order = jnp.cumsum(mine.astype(jnp.int32), axis=1) - 1
    hit = mine & (order == jnp.arange(4, dtype=jnp.int32))
    returned = jnp.sum(jnp.where(hit, (table % local_blocks)[:, :, None] + 1, 0), axis=1) - 1
    returned = returned.reshape(-1)

    sender = edge_sender.reshape(edge_blocks, slot_count)
    receiver = edge_receiver.reshape(edge_blocks, slot_count)
    lanes = jnp.arange(block_rows, dtype=jnp.int32)
    live = jnp.arange(slot_count, dtype=jnp.int32)[None, :] < edge_live[:, None]
    send_hot = (sender[:, :, None] == lanes).astype(BF16)
    receive_hot = ((receiver[:, :, None] == lanes) & live[:, :, None]).astype(BF16)
    adj = jnp.einsum("ker,ket->krt", receive_hot, send_hot, preferred_element_type=F32).astype(BF16)

    after, adj, tile, slot, flipped, out_place, returned = order_together(
        after, adj, tile, slot, flipped, out_place, returned
    )
    xs = [own, other_own, after, send_y(after, 0, 1), *far]
    xs += [*(send_y(v, 0, 1) for v in far), before, send_y(before, 0, 1)]

    x_sel, slope, *parts = edge_forward(my_z.reshape(1), tile, slot, xs, adj, weight_in, bias_in)

    z_sums = scatter_z_ring(parts[NX:])
    x_sums = scatter_x_twice(parts[:NX])
    agg_a = exchange_z(x_sums).astype(F32).sum(0)
    agg_b = scatter_x([z_sums[r] for r in range(NX)], F32)

    mesh_out, u_a, u_b, active, agg, d_agg = node_step(
        agg_a, agg_b, mesh_lat, cotangent, weight_out, weight_node, norm_gain
    )
    u_b = jnp.stack([u_b] + [send_x(u_b, -k) for k in range(1, NX)])
    u_a = exchange_z(jnp.broadcast_to(u_a[None], (NZ, block_rows, HALF)))
    u_a = gather_x_twice(u_a)
    u_b = gather_z_ring(u_b)

    d_pre, *back = edge_backward(slot, flipped, out_place, u_a, u_b, adj, slope)

    in_term = transposed_times(
        x_sel.reshape(edge_blocks * block_rows, width), d_pre.reshape(edge_blocks * block_rows, width)
    )
    node_term, out_term = transposed_times(active, cotangent), transposed_times(agg, d_agg)
    sums = jnp.concatenate([in_term, out_term, node_term], axis=1).astype(BF16)

    got = [back[0]] + [None] * (MESH_N - 1)
    for k in (0, 2, 1, 3):
        for c in range(2):
            if k or c:
                got[((NY - k) % NY) * 2 + c] = send_y(back[k * 2 + c], k, c)
    sums = reduce_core(sums, my_core)
    sums, got[1] = order_together(sums, got[1])
    sums = reduce_y(sums, my_y)
    sums, got[4] = order_together(sums, got[4])
    sums = reduce_grid(sums.reshape(-1, sums.shape[-1]))
    sums, got[5] = order_together(sums, got[5])
    sums = spread_grid(sums)
    sums, got[6], got[2] = order_together(sums, got[6], got[2])
    sums = spread_y(sums)
    sums, got[7], got[3] = order_together(sums, got[7], got[3])
    others = send_y(sums, 0, 1)

    grid_grad = row_step(returned, got, weight_in, local_blocks)

    by_edge = 1.0 / math.sqrt(edge_blocks * slot_count * GRID_N * MESH_N)
    by_node = 1.0 / math.sqrt(block_rows * GRID_N * MESH_N)
    me = jnp.stack([my_y, my_core]).astype(jnp.int32)
    grad_in, grad_out, grad_node = finish(me, sums, others, width, (by_edge, by_edge, by_node))
    return (mesh_out, grid_grad, grad_in, grad_out, grad_node)


def solution(mesh):
    rows = P(("grid", "mesh"), None)
    line = P(("grid", "mesh"))
    return jax.shard_map(
        shards,
        mesh=mesh,
        in_specs=(rows, rows, line, line, line, line, line, P(), P(), P(), P(), P(), rows),
        out_specs=(rows, rows, P(), P(), P()),
        check_vma=False,
    )
```

```python
import math

import jax
import jax.numpy as jnp
from jax import lax
from jax.experimental import pallas as pl
from jax.experimental.pallas import tpu as pltpu
from jax.sharding import PartitionSpec as P

EPSILON = 1e-05
F32, BF16 = jnp.float32, jnp.bfloat16
NX, NZ, NY = 4, 8, 4
GRID_N, MESH_N = NX * NZ, 2 * NY
HALF = 256
VMEM = pl.BlockSpec(memory_space=pltpu.VMEM)
SMEM = pl.BlockSpec(memory_space=pltpu.SMEM)


def sigmoid(v):
    return 0.5 + 0.5 * jnp.tanh(0.5 * v)


def kernel_params(mib):
    return pltpu.CompilerParams(vmem_limit_bytes=mib * 1024 * 1024)


def send_y(v, k, c=0):
    pairs = [(m, ((m // 2 + k) % NY) * 2 + ((m % 2) ^ c)) for m in range(MESH_N)]
    return lax.ppermute(v, "mesh", pairs)


def send_x(v, k):
    return lax.ppermute(v, "grid", [(g, ((g // NZ + k) % NX) * NZ + g % NZ) for g in range(GRID_N)])


def send_z(v, k):
    return lax.ppermute(v, "grid", [(g, (g // NZ) * NZ + (g % NZ + k) % NZ) for g in range(GRID_N)])


def order_together(*values):
    return lax.optimization_barrier(values)


def total(parts, dtype=BF16):
    t = parts[0].astype(F32)
    for p in parts[1:]:
        t = t + p.astype(F32)
    return t.astype(dtype)


def join(*parts):
    return jnp.concatenate(parts, axis=0)


def scatter_x(parts, dtype=BF16):
    return total([parts[0]] + [send_x(parts[k], k) for k in (1, 3, 2)], dtype)


def scatter_x_twice(parts):
    h = parts[2].shape[0] // 2
    up, down = send_x(parts[2][:h], 1), send_x(parts[2][h:], -1)
    up = send_x(join(total([up, parts[1][:h]]), parts[1][h:]), 1)
    down = send_x(join(parts[3][:h], total([down, parts[3][h:]])), -1)
    return total([parts[0], up, down])


def exchange_z(v):
    rows = [[x * NZ + z for z in range(NZ)] for x in range(NX)]
    return lax.all_to_all(v, "grid", 0, 0, axis_index_groups=rows)


def gather_x_twice(v):
    h = v.shape[0] // 2
    up, down = send_x(v, 1), send_x(v, -1)
    return [v, down, send_x(down[:h], -1), send_x(up[h:], 1), up]


def scatter_z_ring(parts):
    up, down = send_z(parts[3], 1), send_z(parts[4], -1)
    up, down = total([up, parts[2]]), total([down, parts[5]])
    up, down = send_z(up, 1), send_z(down, -1)
    up, down = total([up, parts[1]]), total([down, parts[6]])
    up, down = send_z(up, 1), send_z(down, -1)
    down = send_z(total([down, parts[7]]), -1)
    return total([parts[0], up, down])


def gather_z_ring(v):
    out = [v] + [None] * (NZ - 1)
    up = down = v
    for k in range(1, 5):
        if k < 4:
            up = send_z(up, 1)
            out[NZ - k] = up
        down = send_z(down, -1)
        out[k] = down
    return out


def select_tile(index, arrays, write):
    start = 0
    for ref in arrays:
        lo, hi = start, start + ref.shape[0]

        @pl.when((index >= lo) & (index < hi))
        def _():
            write(ref, index - lo)

        start = hi


def edge_forward_kernel(me, tile, slot, *refs):
    refs, outs, part = refs[: -NX - NZ - 1], refs[-NX - NZ - 1 : -1], refs[-1]
    *xs, adj, w_in, bias, x_sel, slope = refs
    part[...] = jnp.zeros_like(part)
    count = adj.shape[0]

    def step(i, _):
        for r in range(2):
            j = 2 * i + r

            def write(ref, place):
                x_sel[j] = ref[place]

            select_tile(tile[j], xs, write)
        rows = x_sel[pl.ds(2 * i, 2)]
        rows = rows.reshape(2 * rows.shape[1], rows.shape[2])
        pre = jnp.dot(rows, w_in[...], preferred_element_type=F32) + bias[...]
        gate = sigmoid(pre)
        hidden = (pre * gate).astype(BF16)
        rise = (gate * (1.0 + pre * (1.0 - gate))).astype(BF16)
        for r in range(2):
            j = 2 * i + r
            slope[j] = rise[r * 128 : (r + 1) * 128]
            term = jnp.dot(adj[j], hidden[r * 128 : (r + 1) * 128], preferred_element_type=F32)
            part[slot[j]] += term
        return 0

    lax.fori_loop(0, count // 2, step, 0, unroll=2)
    for a in range(NX):
        outs[a][...] = part[a * NZ : (a + 1) * NZ, :, :HALF].astype(BF16)
    for r in range(NZ):
        for a in range(NX):
            outs[NX + r][a] = part[a * NZ + lax.rem(me[0] + r, NZ), :, HALF:].astype(BF16)


def edge_forward(me, tile, slot, xs, adj, w_in, bias):
    count, rows, width = adj.shape[0], xs[0].shape[1], xs[0].shape[2]
    block = jax.ShapeDtypeStruct((count, rows, width), BF16)
    by_x = jax.ShapeDtypeStruct((NZ, rows, HALF), BF16)
    by_z = jax.ShapeDtypeStruct((NX, rows, width - HALF), BF16)
    return pl.pallas_call(
        edge_forward_kernel,
        out_shape=(block, block) + (by_x,) * NX + (by_z,) * NZ,
        in_specs=[SMEM] * 3 + [VMEM] * (len(xs) + 3),
        out_specs=(VMEM,) * (2 + NX + NZ),
        scratch_shapes=[pltpu.VMEM((GRID_N, rows, width), F32)],
        compiler_params=kernel_params(28),
        name="edge_forward",
    )(me, tile, slot, *xs, adj, w_in, bias.reshape(1, -1))


def times_transposed(a, b):
    return lax.dot_general(a, b, (((1,), (1,)), ((), ())), preferred_element_type=F32)


def transposed_times(a, b):
    return lax.dot_general(a, b, (((0,), (0,)), ((), ())), preferred_element_type=F32)


def node_kernel(
    agg_a, agg_b, mesh_lat, cot, w_out, w_node, gain, mesh_out, u_a, u_b, active_out, agg_out, d_agg_out
):
    agg = jnp.concatenate([agg_a[...], agg_b[...]], axis=1)
    high = agg.astype(BF16)
    low = (agg - high.astype(F32)).astype(BF16)
    aggregate = jnp.dot(high, w_out[...], preferred_element_type=F32) + jnp.dot(
        low, w_out[...], preferred_element_type=F32
    )
    summed = mesh_lat[...].astype(F32) + aggregate
    centred = summed - jnp.mean(summed, axis=-1, keepdims=True)
    inverse = lax.rsqrt(jnp.mean(centred * centred, axis=-1, keepdims=True) + EPSILON)
    standard = centred * inverse
    normed = standard * gain[...]
    gate = sigmoid(normed)
    active = (normed * gate).astype(BF16)
    mesh_out[...] = (summed + jnp.dot(active, w_node[...], preferred_element_type=F32)).astype(BF16)
    d_active = times_transposed(cot[...], w_node[...])
    d_standard = d_active * (gate * (1.0 + normed * (1.0 - gate))) * gain[...]
    first = jnp.mean(d_standard, axis=-1, keepdims=True)
    second = jnp.mean(d_standard * standard, axis=-1, keepdims=True)
    d_summed = cot[...].astype(F32) + inverse * (d_standard - first - standard * second)
    d_agg = d_summed.astype(BF16)
    u = times_transposed(d_agg, w_out[...]).astype(BF16)
    u_a[...] = u[:, :HALF]
    u_b[...] = u[:, HALF:]
    active_out[...] = active
    agg_out[...] = high
    d_agg_out[...] = d_agg


def node_step(agg_a, agg_b, mesh_lat, cot, w_out, w_node, gain):
    rows, width = mesh_lat.shape
    whole = jax.ShapeDtypeStruct((rows, width), BF16)
    return pl.pallas_call(
        node_kernel,
        out_shape=(
            whole,
            jax.ShapeDtypeStruct((rows, HALF), BF16),
            jax.ShapeDtypeStruct((rows, width - HALF), BF16),
            whole,
            whole,
            whole,
        ),
        in_specs=[VMEM] * 7,
        out_specs=(VMEM,) * 6,
        compiler_params=kernel_params(12),
        name="node_step",
    )(agg_a, agg_b, mesh_lat, cot, w_out, w_node, gain.reshape(1, -1))


def edge_backward_kernel(slot, flipped, out_place, *refs):
    refs, outs, (u_first, u_second, back) = refs[: -MESH_N - 3], refs[-MESH_N - 3 : -3], refs[-3:]
    *refs, adj, slope, d_pre = refs
    for scratch, pieces in ((u_first, refs[:-NZ]), (u_second, refs[-NZ:])):
        start = 0
        for ref in pieces:
            scratch[start : start + ref.shape[0]] = ref[...]
            start += ref.shape[0]

    def step(j, _):
        u = jnp.concatenate([u_first[slot[j]], u_second[flipped[j]]], axis=1)
        term = (transposed_times(adj[j], u) * slope[j].astype(F32)).astype(BF16)
        d_pre[j] = term
        back[out_place[j]] = term
        return 0

    lax.fori_loop(0, adj.shape[0], step, 0, unroll=4)
    for i, ref in enumerate(outs):
        ref[...] = back[4 * i : 4 * (i + 1)]


def edge_backward(slot, flipped, out_place, u_a, u_b, adj, slope):
    count, rows, width = slope.shape
    return pl.pallas_call(
        edge_backward_kernel,
        out_shape=(jax.ShapeDtypeStruct(slope.shape, BF16),)
        + (jax.ShapeDtypeStruct((4, rows, width), BF16),) * MESH_N,
        in_specs=[SMEM] * 3 + [VMEM] * (len(u_a) + len(u_b) + 2),
        out_specs=(VMEM,) * (1 + MESH_N),
        scratch_shapes=[
            pltpu.VMEM((GRID_N, rows, HALF), BF16),
            pltpu.VMEM((GRID_N, rows, width - HALF), BF16),
            pltpu.VMEM((4 * MESH_N, rows, width), BF16),
        ],
        compiler_params=kernel_params(26),
        name="edge_backward",
    )(slot, flipped, out_place, *u_a, *u_b, adj, slope)


def row_kernel(place, *refs):
    parts = refs[:MESH_N]
    w_in, out, acc = refs[MESH_N:]
    acc[...] = jnp.zeros_like(acc)
    for s, ref in enumerate(parts):
        for q in range(4):

            @pl.when(place[s * 4 + q] >= 0)
            def _():
                acc[place[s * 4 + q]] += ref[q].astype(F32)

    blocks, rows, width = acc.shape
    for i in range(0, blocks, 2):
        row_sum = acc[i : i + 2].reshape(2 * rows, width).astype(BF16)
        out[i * rows : (i + 2) * rows] = times_transposed(row_sum, w_in[...]).astype(BF16)


def row_step(place, parts, w_in, blocks):
    _, rows, width = parts[0].shape
    return pl.pallas_call(
        row_kernel,
        out_shape=jax.ShapeDtypeStruct((blocks * rows, width), BF16),
        in_specs=[SMEM] + [VMEM] * (MESH_N + 1),
        out_specs=VMEM,
        scratch_shapes=[pltpu.VMEM((blocks, rows, width), F32)],
        compiler_params=kernel_params(16),
        name="row_step",
    )(place, *parts, w_in)


def pick(v, index):
    return lax.dynamic_index_in_dim(v, index, 0, keepdims=False)


def reduce_core(v, my_core):
    rows, width = v.shape
    v = v.reshape(NY, 2, rows // MESH_N, width)
    keep = lax.dynamic_index_in_dim(v, my_core, 1, keepdims=False)
    return total([keep, send_y(lax.dynamic_index_in_dim(v, 1 - my_core, 1, keepdims=False), 0, 1)])


def reduce_y(v, my_y):
    parts = [pick(v, (my_y + k) % NY) for k in range(NY)]
    return total([parts[0]] + [send_y(parts[k], k, 0) for k in (2, 1, 3)])


def reduce_grid(v):
    rows, width = v.shape
    v = lax.all_to_all(v.reshape(GRID_N, rows // GRID_N, width), "grid", 0, 0)
    return v.astype(F32).sum(0).astype(BF16)


def spread_grid(v):
    rows, width = v.shape
    v = lax.all_to_all(jnp.broadcast_to(v[None], (GRID_N, rows, width)), "grid", 0, 0)
    return v.reshape(GRID_N * rows, width)


def spread_y(v):
    return jnp.stack([v] + [send_y(v, -k, 0) for k in (1, 2, 3)])


def finish_kernel(scales, me, mine, other, *outs):
    run = mine.shape[1]
    width = outs[0].shape[1]
    for k in range(NY):
        y = lax.rem(me[0] + k, NY)
        for ref, core in ((mine, me[1]), (other, 1 - me[1])):
            rows = pl.ds(pl.multiple_of((2 * y + core) * run, run), run)
            for i, out in enumerate(outs):
                out[rows, :] = ref[k, :, i * width : (i + 1) * width].astype(F32) * scales[i]


def finish(me, mine, other, width, scales):
    return pl.pallas_call(
        lambda *refs: finish_kernel(scales, *refs),
        out_shape=(jax.ShapeDtypeStruct((width, width), F32),) * 3,
        in_specs=[SMEM, VMEM, VMEM],
        out_specs=(VMEM,) * 3,
        compiler_params=kernel_params(12),
        name="finish",
    )(me, mine, other)


def shards(
    grid_lat,
    mesh_lat,
    edge_grid_block,
    edge_mesh_block,
    edge_sender,
    edge_receiver,
    edge_live,
    weight_in,
    bias_in,
    weight_out,
    norm_gain,
    weight_node,
    cotangent,
):
    block_rows, width = mesh_lat.shape
    local_blocks = grid_lat.shape[0] // block_rows
    edge_blocks = edge_grid_block.shape[0]
    slot_count = edge_sender.shape[0] // edge_blocks
    g, m = lax.axis_index("grid"), lax.axis_index("mesh")
    my_x, my_z, my_y, my_core = g // NZ, g % NZ, m // 2, m % 2

    holder, place = edge_grid_block // local_blocks, edge_grid_block % local_blocks
    rel_holder = ((holder // 2 - my_y) % NY) * 2 + ((holder % 2) ^ my_core)
    tile = rel_holder * local_blocks + place
    rel_x, rel_z = (edge_mesh_block // NZ - my_x) % NX, (edge_mesh_block % NZ - my_z) % NZ
    slot, flipped = rel_x * NZ + edge_mesh_block % NZ, rel_z * NX + rel_x
    earlier = jnp.arange(edge_blocks)[None, :] < jnp.arange(edge_blocks)[:, None]
    rank = jnp.sum((rel_holder[:, None] == rel_holder[None, :]) & earlier, axis=1).astype(jnp.int32)
    out_place = rel_holder * 4 + rank

    own = grid_lat.reshape(local_blocks, block_rows, width)
    half = local_blocks // 2
    after, before = send_y(own, -1), send_y(own, 1)
    far = [send_y(before[:half], 1), send_y(after[half:], -1)]
    other_own, blocks = order_together(send_y(own, 0, 1), edge_grid_block)

    table = jnp.stack([blocks] + [send_y(blocks, -k, 0) for k in (1, 2, 3)])
    table = jnp.stack([table, send_y(table, 0, 1)], axis=1).reshape(MESH_N, edge_blocks)
    mine = (table // local_blocks == m)[:, :, None]
    order = jnp.cumsum(mine.astype(jnp.int32), axis=1) - 1
    hit = mine & (order == jnp.arange(4, dtype=jnp.int32))
    returned = jnp.sum(jnp.where(hit, (table % local_blocks)[:, :, None] + 1, 0), axis=1) - 1
    returned = returned.reshape(-1)

    sender = edge_sender.reshape(edge_blocks, slot_count)
    receiver = edge_receiver.reshape(edge_blocks, slot_count)
    lanes = jnp.arange(block_rows, dtype=jnp.int32)
    live = jnp.arange(slot_count, dtype=jnp.int32)[None, :] < edge_live[:, None]
    send_hot = (sender[:, :, None] == lanes).astype(BF16)
    receive_hot = ((receiver[:, :, None] == lanes) & live[:, :, None]).astype(BF16)
    adj = jnp.einsum("ker,ket->krt", receive_hot, send_hot, preferred_element_type=F32).astype(BF16)

    after, adj, tile, slot, flipped, out_place, returned = order_together(
        after, adj, tile, slot, flipped, out_place, returned
    )
    xs = [own, other_own, after, send_y(after, 0, 1), *far]
    xs += [*(send_y(v, 0, 1) for v in far), before, send_y(before, 0, 1)]

    x_sel, slope, *parts = edge_forward(my_z.reshape(1), tile, slot, xs, adj, weight_in, bias_in)

    z_sums = scatter_z_ring(parts[NX:])
    x_sums = scatter_x_twice(parts[:NX])
    agg_a = exchange_z(x_sums).astype(F32).sum(0)
    agg_b = scatter_x([z_sums[r] for r in range(NX)], F32)

    mesh_out, u_a, u_b, active, agg, d_agg = node_step(
        agg_a, agg_b, mesh_lat, cotangent, weight_out, weight_node, norm_gain
    )
    u_b = jnp.stack([u_b] + [send_x(u_b, -k) for k in range(1, NX)])
    u_a = exchange_z(jnp.broadcast_to(u_a[None], (NZ, block_rows, HALF)))
    u_a = gather_x_twice(u_a)
    u_b = gather_z_ring(u_b)

    d_pre, *back = edge_backward(slot, flipped, out_place, u_a, u_b, adj, slope)

    in_term = transposed_times(
        x_sel.reshape(edge_blocks * block_rows, width), d_pre.reshape(edge_blocks * block_rows, width)
    )
    node_term, out_term = transposed_times(active, cotangent), transposed_times(agg, d_agg)
    sums = jnp.concatenate([in_term, out_term, node_term], axis=1).astype(BF16)

    got = [back[0]] + [None] * (MESH_N - 1)
    for k in (0, 2, 1, 3):
        for c in range(2):
            if k or c:
                got[((NY - k) % NY) * 2 + c] = send_y(back[k * 2 + c], k, c)
    sums = reduce_core(sums, my_core)
    sums, got[1] = order_together(sums, got[1])
    sums = reduce_y(sums, my_y)
    sums = reduce_grid(sums.reshape(-1, sums.shape[-1]))
    sums, got[4], got[5] = order_together(sums, got[4], got[5])
    sums = spread_grid(sums)
    sums, got[6], got[2] = order_together(sums, got[6], got[2])
    sums = spread_y(sums)
    sums, got[7], got[3] = order_together(sums, got[7], got[3])
    others = send_y(sums, 0, 1)

    grid_grad = row_step(returned, got, weight_in, local_blocks)

    by_edge = 1.0 / math.sqrt(edge_blocks * slot_count * GRID_N * MESH_N)
    by_node = 1.0 / math.sqrt(block_rows * GRID_N * MESH_N)
    me = jnp.stack([my_y, my_core]).astype(jnp.int32)
    grad_in, grad_out, grad_node = finish(me, sums, others, width, (by_edge, by_edge, by_node))
    return (mesh_out, grid_grad, grad_in, grad_out, grad_node)


def solution(mesh):
    rows = P(("grid", "mesh"), None)
    line = P(("grid", "mesh"))
    return jax.shard_map(
        shards,
        mesh=mesh,
        in_specs=(rows, rows, line, line, line, line, line, P(), P(), P(), P(), P(), rows),
        out_specs=(rows, rows, P(), P(), P()),
        check_vma=False,
    )
```

```python
import math

import jax
import jax.numpy as jnp
from jax import lax
from jax.experimental import pallas as pl
from jax.experimental.pallas import tpu as pltpu
from jax.sharding import PartitionSpec as P

EPSILON = 1e-05
F32, BF16 = jnp.float32, jnp.bfloat16
NX, NZ, NY = 4, 8, 4
GRID_N, MESH_N = NX * NZ, 2 * NY
HALF = 256
VMEM = pl.BlockSpec(memory_space=pltpu.VMEM)
SMEM = pl.BlockSpec(memory_space=pltpu.SMEM)


def sigmoid(v):
    return 0.5 + 0.5 * jnp.tanh(0.5 * v)


def kernel_params(mib):
    return pltpu.CompilerParams(vmem_limit_bytes=mib * 1024 * 1024)


def send_y(v, k, c=0):
    pairs = [(m, ((m // 2 + k) % NY) * 2 + ((m % 2) ^ c)) for m in range(MESH_N)]
    return lax.ppermute(v, "mesh", pairs)


def send_x(v, k):
    return lax.ppermute(v, "grid", [(g, ((g // NZ + k) % NX) * NZ + g % NZ) for g in range(GRID_N)])


def send_z(v, k):
    return lax.ppermute(v, "grid", [(g, (g // NZ) * NZ + (g % NZ + k) % NZ) for g in range(GRID_N)])


def order_together(*values):
    return lax.optimization_barrier(values)


def total(parts, dtype=BF16):
    t = parts[0].astype(F32)
    for p in parts[1:]:
        t = t + p.astype(F32)
    return t.astype(dtype)


def join(*parts):
    return jnp.concatenate(parts, axis=0)


def scatter_x(parts, dtype=BF16):
    return total([parts[0]] + [send_x(parts[k], k) for k in (1, 3, 2)], dtype)


def scatter_x_twice(parts):
    h = parts[2].shape[0] // 2
    up, down = send_x(parts[2][:h], 1), send_x(parts[2][h:], -1)
    up = send_x(join(total([up, parts[1][:h]]), parts[1][h:]), 1)
    down = send_x(join(parts[3][:h], total([down, parts[3][h:]])), -1)
    return total([parts[0], up, down])


def exchange_z(v):
    rows = [[x * NZ + z for z in range(NZ)] for x in range(NX)]
    return lax.all_to_all(v, "grid", 0, 0, axis_index_groups=rows)


def gather_x_twice(v):
    h = v.shape[0] // 2
    up, down = send_x(v, 1), send_x(v, -1)
    return [v, down, send_x(down[:h], -1), send_x(up[h:], 1), up]


def scatter_z_ring(parts):
    up, down = send_z(parts[3], 1), send_z(parts[4], -1)
    up, down = total([up, parts[2]]), total([down, parts[5]])
    up, down = send_z(up, 1), send_z(down, -1)
    up, down = total([up, parts[1]]), total([down, parts[6]])
    up, down = send_z(up, 1), send_z(down, -1)
    down = send_z(total([down, parts[7]]), -1)
    return total([parts[0], up, down])


def gather_z_ring(v):
    out = [v] + [None] * (NZ - 1)
    up = down = v
    for k in range(1, 5):
        if k < 4:
            up = send_z(up, 1)
            out[NZ - k] = up
        down = send_z(down, -1)
        out[k] = down
    return out


def select_tile(index, arrays, write):
    start = 0
    for ref in arrays:
        lo, hi = start, start + ref.shape[0]

        @pl.when((index >= lo) & (index < hi))
        def _():
            write(ref, index - lo)

        start = hi


def edge_forward_kernel(me, tile, slot, *refs):
    refs, outs, part = refs[: -NX - NZ - 1], refs[-NX - NZ - 1 : -1], refs[-1]
    *xs, adj, w_in, bias, x_sel, slope = refs
    part[...] = jnp.zeros_like(part)
    count = adj.shape[0]

    def step(i, _):
        for r in range(2):
            j = 2 * i + r

            def write(ref, place):
                x_sel[j] = ref[place]

            select_tile(tile[j], xs, write)
        rows = x_sel[pl.ds(2 * i, 2)]
        rows = rows.reshape(2 * rows.shape[1], rows.shape[2])
        pre = jnp.dot(rows, w_in[...], preferred_element_type=F32) + bias[...]
        gate = sigmoid(pre)
        hidden = (pre * gate).astype(BF16)
        rise = (gate * (1.0 + pre * (1.0 - gate))).astype(BF16)
        for r in range(2):
            j = 2 * i + r
            slope[j] = rise[r * 128 : (r + 1) * 128]
            term = jnp.dot(adj[j], hidden[r * 128 : (r + 1) * 128], preferred_element_type=F32)
            part[slot[j]] += term
        return 0

    lax.fori_loop(0, count // 2, step, 0, unroll=2)
    for a in range(NX):
        outs[a][...] = part[a * NZ : (a + 1) * NZ, :, :HALF].astype(BF16)
    for r in range(NZ):
        for a in range(NX):
            outs[NX + r][a] = part[a * NZ + lax.rem(me[0] + r, NZ), :, HALF:].astype(BF16)


def edge_forward(me, tile, slot, xs, adj, w_in, bias):
    count, rows, width = adj.shape[0], xs[0].shape[1], xs[0].shape[2]
    block = jax.ShapeDtypeStruct((count, rows, width), BF16)
    by_x = jax.ShapeDtypeStruct((NZ, rows, HALF), BF16)
    by_z = jax.ShapeDtypeStruct((NX, rows, width - HALF), BF16)
    return pl.pallas_call(
        edge_forward_kernel,
        out_shape=(block, block) + (by_x,) * NX + (by_z,) * NZ,
        in_specs=[SMEM] * 3 + [VMEM] * (len(xs) + 3),
        out_specs=(VMEM,) * (2 + NX + NZ),
        scratch_shapes=[pltpu.VMEM((GRID_N, rows, width), F32)],
        compiler_params=kernel_params(28),
        name="edge_forward",
    )(me, tile, slot, *xs, adj, w_in, bias.reshape(1, -1))


def times_transposed(a, b):
    return lax.dot_general(a, b, (((1,), (1,)), ((), ())), preferred_element_type=F32)


def transposed_times(a, b):
    return lax.dot_general(a, b, (((0,), (0,)), ((), ())), preferred_element_type=F32)


def node_kernel(
    agg_a, agg_b, mesh_lat, cot, w_out, w_node, gain, mesh_out, u_a, u_b, active_out, agg_out, d_agg_out
):
    agg = jnp.concatenate([agg_a[...], agg_b[...]], axis=1)
    high = agg.astype(BF16)
    low = (agg - high.astype(F32)).astype(BF16)
    aggregate = jnp.dot(high, w_out[...], preferred_element_type=F32) + jnp.dot(
        low, w_out[...], preferred_element_type=F32
    )
    summed = mesh_lat[...].astype(F32) + aggregate
    centred = summed - jnp.mean(summed, axis=-1, keepdims=True)
    inverse = lax.rsqrt(jnp.mean(centred * centred, axis=-1, keepdims=True) + EPSILON)
    standard = centred * inverse
    normed = standard * gain[...]
    gate = sigmoid(normed)
    active = (normed * gate).astype(BF16)
    mesh_out[...] = (summed + jnp.dot(active, w_node[...], preferred_element_type=F32)).astype(BF16)
    d_active = times_transposed(cot[...], w_node[...])
    d_standard = d_active * (gate * (1.0 + normed * (1.0 - gate))) * gain[...]
    first = jnp.mean(d_standard, axis=-1, keepdims=True)
    second = jnp.mean(d_standard * standard, axis=-1, keepdims=True)
    d_summed = cot[...].astype(F32) + inverse * (d_standard - first - standard * second)
    d_agg = d_summed.astype(BF16)
    u = times_transposed(d_agg, w_out[...]).astype(BF16)
    u_a[...] = u[:, :HALF]
    u_b[...] = u[:, HALF:]
    active_out[...] = active
    agg_out[...] = high
    d_agg_out[...] = d_agg


def node_step(agg_a, agg_b, mesh_lat, cot, w_out, w_node, gain):
    rows, width = mesh_lat.shape
    whole = jax.ShapeDtypeStruct((rows, width), BF16)
    return pl.pallas_call(
        node_kernel,
        out_shape=(
            whole,
            jax.ShapeDtypeStruct((rows, HALF), BF16),
            jax.ShapeDtypeStruct((rows, width - HALF), BF16),
            whole,
            whole,
            whole,
        ),
        in_specs=[VMEM] * 7,
        out_specs=(VMEM,) * 6,
        compiler_params=kernel_params(12),
        name="node_step",
    )(agg_a, agg_b, mesh_lat, cot, w_out, w_node, gain.reshape(1, -1))


def edge_backward_kernel(slot, flipped, out_place, *refs):
    refs, outs, (u_first, u_second, back) = refs[: -MESH_N - 3], refs[-MESH_N - 3 : -3], refs[-3:]
    *refs, adj, slope, d_pre = refs
    for scratch, pieces in ((u_first, refs[:-NZ]), (u_second, refs[-NZ:])):
        start = 0
        for ref in pieces:
            scratch[start : start + ref.shape[0]] = ref[...]
            start += ref.shape[0]

    def step(j, _):
        u = jnp.concatenate([u_first[slot[j]], u_second[flipped[j]]], axis=1)
        term = (transposed_times(adj[j], u) * slope[j].astype(F32)).astype(BF16)
        d_pre[j] = term
        back[out_place[j]] = term
        return 0

    lax.fori_loop(0, adj.shape[0], step, 0, unroll=4)
    for i, ref in enumerate(outs):
        ref[...] = back[4 * i : 4 * (i + 1)]


def edge_backward(slot, flipped, out_place, u_a, u_b, adj, slope):
    count, rows, width = slope.shape
    return pl.pallas_call(
        edge_backward_kernel,
        out_shape=(jax.ShapeDtypeStruct(slope.shape, BF16),)
        + (jax.ShapeDtypeStruct((4, rows, width), BF16),) * MESH_N,
        in_specs=[SMEM] * 3 + [VMEM] * (len(u_a) + len(u_b) + 2),
        out_specs=(VMEM,) * (1 + MESH_N),
        scratch_shapes=[
            pltpu.VMEM((GRID_N, rows, HALF), BF16),
            pltpu.VMEM((GRID_N, rows, width - HALF), BF16),
            pltpu.VMEM((4 * MESH_N, rows, width), BF16),
        ],
        compiler_params=kernel_params(26),
        name="edge_backward",
    )(slot, flipped, out_place, *u_a, *u_b, adj, slope)


def row_kernel(place, *refs):
    parts = refs[:MESH_N]
    w_in, out, acc = refs[MESH_N:]
    acc[...] = jnp.zeros_like(acc)
    for s, ref in enumerate(parts):
        for q in range(4):

            @pl.when(place[s * 4 + q] >= 0)
            def _():
                acc[place[s * 4 + q]] += ref[q].astype(F32)

    blocks, rows, width = acc.shape
    for i in range(0, blocks, 2):
        row_sum = acc[i : i + 2].reshape(2 * rows, width).astype(BF16)
        out[i * rows : (i + 2) * rows] = times_transposed(row_sum, w_in[...]).astype(BF16)


def row_step(place, parts, w_in, blocks):
    _, rows, width = parts[0].shape
    return pl.pallas_call(
        row_kernel,
        out_shape=jax.ShapeDtypeStruct((blocks * rows, width), BF16),
        in_specs=[SMEM] + [VMEM] * (MESH_N + 1),
        out_specs=VMEM,
        scratch_shapes=[pltpu.VMEM((blocks, rows, width), F32)],
        compiler_params=kernel_params(16),
        name="row_step",
    )(place, *parts, w_in)


def pick(v, index):
    return lax.dynamic_index_in_dim(v, index, 0, keepdims=False)


def fold_kernel(me, keep, got, *outs):
    for k, out in enumerate(outs):
        y = lax.rem(me[0] + k, NY)
        out[...] = (keep[y].astype(F32) + got[y].astype(F32)).astype(BF16)


def reduce_core(v, my_y, my_core):
    rows, width = v.shape
    v = v.reshape(NY, 2, rows // MESH_N, width)
    keep = lax.dynamic_index_in_dim(v, my_core, 1, keepdims=False)
    got = send_y(lax.dynamic_index_in_dim(v, 1 - my_core, 1, keepdims=False), 0, 1)
    return pl.pallas_call(
        fold_kernel,
        out_shape=(jax.ShapeDtypeStruct((rows // MESH_N, width), BF16),) * NY,
        in_specs=[SMEM, VMEM, VMEM],
        out_specs=(VMEM,) * NY,
        compiler_params=kernel_params(8),
        name="fold",
    )(my_y.reshape(1), keep, got)


def shares_kernel(*refs):
    *parts, out = refs
    count, run, _ = out.shape
    t = parts[0][...].astype(F32)
    for p in parts[1:]:
        t = t + p[...].astype(F32)
    for i in range(count):
        out[i] = t[i * run : (i + 1) * run].astype(BF16)


def reduce_y(parts):
    rows, width = parts[0].shape
    parts = [parts[0]] + [send_y(parts[k], k, 0) for k in (2, 1, 3)]
    return pl.pallas_call(
        shares_kernel,
        out_shape=jax.ShapeDtypeStruct((GRID_N, rows // GRID_N, width), BF16),
        in_specs=[VMEM] * NY,
        out_specs=VMEM,
        compiler_params=kernel_params(8),
        name="shares",
    )(*parts)


def reduce_grid(v):
    return lax.all_to_all(v, "grid", 0, 0).astype(F32).sum(0).astype(BF16)


def spread_grid(v):
    rows, width = v.shape
    v = lax.all_to_all(jnp.broadcast_to(v[None], (GRID_N, rows, width)), "grid", 0, 0)
    return v.reshape(GRID_N * rows, width)


def spread_y(v):
    return jnp.stack([v] + [send_y(v, -k, 0) for k in (1, 2, 3)])


def finish_kernel(scales, me, mine, other, *outs):
    run = mine.shape[1]
    width = outs[0].shape[1]
    for k in range(NY):
        y = lax.rem(me[0] + k, NY)
        for ref, core in ((mine, me[1]), (other, 1 - me[1])):
            rows = pl.ds(pl.multiple_of((2 * y + core) * run, run), run)
            for i, out in enumerate(outs):
                out[rows, :] = ref[k, :, i * width : (i + 1) * width].astype(F32) * scales[i]


def finish(me, mine, other, width, scales):
    return pl.pallas_call(
        lambda *refs: finish_kernel(scales, *refs),
        out_shape=(jax.ShapeDtypeStruct((width, width), F32),) * 3,
        in_specs=[SMEM, VMEM, VMEM],
        out_specs=(VMEM,) * 3,
        compiler_params=kernel_params(12),
        name="finish",
    )(me, mine, other)


def shards(
    grid_lat,
    mesh_lat,
    edge_grid_block,
    edge_mesh_block,
    edge_sender,
    edge_receiver,
    edge_live,
    weight_in,
    bias_in,
    weight_out,
    norm_gain,
    weight_node,
    cotangent,
):
    block_rows, width = mesh_lat.shape
    local_blocks = grid_lat.shape[0] // block_rows
    edge_blocks = edge_grid_block.shape[0]
    slot_count = edge_sender.shape[0] // edge_blocks
    g, m = lax.axis_index("grid"), lax.axis_index("mesh")
    my_x, my_z, my_y, my_core = g // NZ, g % NZ, m // 2, m % 2

    holder, place = edge_grid_block // local_blocks, edge_grid_block % local_blocks
    rel_holder = ((holder // 2 - my_y) % NY) * 2 + ((holder % 2) ^ my_core)
    tile = rel_holder * local_blocks + place
    rel_x, rel_z = (edge_mesh_block // NZ - my_x) % NX, (edge_mesh_block % NZ - my_z) % NZ
    slot, flipped = rel_x * NZ + edge_mesh_block % NZ, rel_z * NX + rel_x
    earlier = jnp.arange(edge_blocks)[None, :] < jnp.arange(edge_blocks)[:, None]
    rank = jnp.sum((rel_holder[:, None] == rel_holder[None, :]) & earlier, axis=1).astype(jnp.int32)
    out_place = rel_holder * 4 + rank

    own = grid_lat.reshape(local_blocks, block_rows, width)
    half = local_blocks // 2
    after, before = send_y(own, -1), send_y(own, 1)
    far = [send_y(before[:half], 1), send_y(after[half:], -1)]
    other_own, blocks = order_together(send_y(own, 0, 1), edge_grid_block)

    table = jnp.stack([blocks] + [send_y(blocks, -k, 0) for k in (1, 2, 3)])
    table = jnp.stack([table, send_y(table, 0, 1)], axis=1).reshape(MESH_N, edge_blocks)
    mine = (table // local_blocks == m)[:, :, None]
    order = jnp.cumsum(mine.astype(jnp.int32), axis=1) - 1
    hit = mine & (order == jnp.arange(4, dtype=jnp.int32))
    returned = jnp.sum(jnp.where(hit, (table % local_blocks)[:, :, None] + 1, 0), axis=1) - 1
    returned = returned.reshape(-1)

    sender = edge_sender.reshape(edge_blocks, slot_count)
    receiver = edge_receiver.reshape(edge_blocks, slot_count)
    lanes = jnp.arange(block_rows, dtype=jnp.int32)
    live = jnp.arange(slot_count, dtype=jnp.int32)[None, :] < edge_live[:, None]
    send_hot = (sender[:, :, None] == lanes).astype(BF16)
    receive_hot = ((receiver[:, :, None] == lanes) & live[:, :, None]).astype(BF16)
    adj = jnp.einsum("ker,ket->krt", receive_hot, send_hot, preferred_element_type=F32).astype(BF16)

    after, adj, tile, slot, flipped, out_place, returned = order_together(
        after, adj, tile, slot, flipped, out_place, returned
    )
    xs = [own, other_own, after, send_y(after, 0, 1), *far]
    xs += [*(send_y(v, 0, 1) for v in far), before, send_y(before, 0, 1)]

    x_sel, slope, *parts = edge_forward(my_z.reshape(1), tile, slot, xs, adj, weight_in, bias_in)

    z_sums = scatter_z_ring(parts[NX:])
    x_sums = scatter_x_twice(parts[:NX])
    agg_a = exchange_z(x_sums).astype(F32).sum(0)
    agg_b = scatter_x([z_sums[r] for r in range(NX)], F32)

    mesh_out, u_a, u_b, active, agg, d_agg = node_step(
        agg_a, agg_b, mesh_lat, cotangent, weight_out, weight_node, norm_gain
    )
    u_b = jnp.stack([u_b] + [send_x(u_b, -k) for k in range(1, NX)])
    u_a = exchange_z(jnp.broadcast_to(u_a[None], (NZ, block_rows, HALF)))
    u_a = gather_x_twice(u_a)
    u_b = gather_z_ring(u_b)

    d_pre, *back = edge_backward(slot, flipped, out_place, u_a, u_b, adj, slope)

    in_term = transposed_times(
        x_sel.reshape(edge_blocks * block_rows, width), d_pre.reshape(edge_blocks * block_rows, width)
    )
    node_term, out_term = transposed_times(active, cotangent), transposed_times(agg, d_agg)
    sums = jnp.concatenate([in_term, out_term, node_term], axis=1).astype(BF16)

    got = [back[0]] + [None] * (MESH_N - 1)
    for k in (0, 2, 1, 3):
        for c in range(2):
            if k or c:
                got[((NY - k) % NY) * 2 + c] = send_y(back[k * 2 + c], k, c)
    sums = reduce_core(sums, my_y, my_core)
    sums = reduce_y(sums)
    sums = reduce_grid(sums)
    sums, got[1], got[4], got[5] = order_together(sums, got[1], got[4], got[5])
    sums = spread_grid(sums)
    sums, got[6], got[2] = order_together(sums, got[6], got[2])
    sums = spread_y(sums)
    sums, got[7], got[3] = order_together(sums, got[7], got[3])
    others = send_y(sums, 0, 1)

    grid_grad = row_step(returned, got, weight_in, local_blocks)

    by_edge = 1.0 / math.sqrt(edge_blocks * slot_count * GRID_N * MESH_N)
    by_node = 1.0 / math.sqrt(block_rows * GRID_N * MESH_N)
    me = jnp.stack([my_y, my_core]).astype(jnp.int32)
    grad_in, grad_out, grad_node = finish(me, sums, others, width, (by_edge, by_edge, by_node))
    return (mesh_out, grid_grad, grad_in, grad_out, grad_node)


def solution(mesh):
    rows = P(("grid", "mesh"), None)
    line = P(("grid", "mesh"))
    return jax.shard_map(
        shards,
        mesh=mesh,
        in_specs=(rows, rows, line, line, line, line, line, P(), P(), P(), P(), P(), rows),
        out_specs=(rows, rows, P(), P(), P()),
        check_vma=False,
    )
```

```python
import math

import jax
import jax.numpy as jnp
from jax import lax
from jax.experimental import pallas as pl
from jax.experimental.pallas import tpu as pltpu
from jax.sharding import PartitionSpec as P

EPSILON = 1e-05
F32, BF16 = jnp.float32, jnp.bfloat16
NX, NZ, NY = 4, 8, 4
GRID_N, MESH_N = NX * NZ, 2 * NY
HALF = 256
VMEM = pl.BlockSpec(memory_space=pltpu.VMEM)
SMEM = pl.BlockSpec(memory_space=pltpu.SMEM)


def sigmoid(v):
    return 0.5 + 0.5 * jnp.tanh(0.5 * v)


def kernel_params(mib):
    return pltpu.CompilerParams(vmem_limit_bytes=mib * 1024 * 1024)


def send_y(v, k, c=0):
    pairs = [(m, ((m // 2 + k) % NY) * 2 + ((m % 2) ^ c)) for m in range(MESH_N)]
    return lax.ppermute(v, "mesh", pairs)


def send_x(v, k):
    return lax.ppermute(v, "grid", [(g, ((g // NZ + k) % NX) * NZ + g % NZ) for g in range(GRID_N)])


def send_z(v, k):
    return lax.ppermute(v, "grid", [(g, (g // NZ) * NZ + (g % NZ + k) % NZ) for g in range(GRID_N)])


def order_together(*values):
    return lax.optimization_barrier(values)


def total(parts, dtype=BF16):
    t = parts[0].astype(F32)
    for p in parts[1:]:
        t = t + p.astype(F32)
    return t.astype(dtype)


def join(*parts):
    return jnp.concatenate(parts, axis=0)


def scatter_x(parts, dtype=BF16):
    return total([parts[0]] + [send_x(parts[k], k) for k in (1, 3, 2)], dtype)


def scatter_x_twice(parts):
    h = parts[2].shape[0] // 2
    up, down = send_x(parts[2][:h], 1), send_x(parts[2][h:], -1)
    up = send_x(join(total([up, parts[1][:h]]), parts[1][h:]), 1)
    down = send_x(join(parts[3][:h], total([down, parts[3][h:]])), -1)
    return total([parts[0], up, down])


def exchange_z(v):
    rows = [[x * NZ + z for z in range(NZ)] for x in range(NX)]
    return lax.all_to_all(v, "grid", 0, 0, axis_index_groups=rows)


def gather_x_twice(v):
    h = v.shape[0] // 2
    up, down = send_x(v, 1), send_x(v, -1)
    return [v, down, send_x(down[:h], -1), send_x(up[h:], 1), up]


def scatter_z_ring(parts):
    up, down = send_z(parts[3], 1), send_z(parts[4], -1)
    up, down = total([up, parts[2]]), total([down, parts[5]])
    up, down = send_z(up, 1), send_z(down, -1)
    up, down = total([up, parts[1]]), total([down, parts[6]])
    up, down = send_z(up, 1), send_z(down, -1)
    down = send_z(total([down, parts[7]]), -1)
    return total([parts[0], up, down])


def gather_z_ring(v):
    out = [v] + [None] * (NZ - 1)
    up = down = v
    for k in range(1, 5):
        if k < 4:
            up = send_z(up, 1)
            out[NZ - k] = up
        down = send_z(down, -1)
        out[k] = down
    return out


def select_tile(index, arrays, write):
    start = 0
    for ref in arrays:
        lo, hi = start, start + ref.shape[0]

        @pl.when((index >= lo) & (index < hi))
        def _():
            write(ref, index - lo)

        start = hi


def edge_forward_kernel(me, tile, slot, *refs):
    refs, outs, part = refs[: -NX - NZ - 1], refs[-NX - NZ - 1 : -1], refs[-1]
    *xs, adj, w_in, bias, x_sel, slope = refs
    part[...] = jnp.zeros_like(part)
    count = adj.shape[0]

    def step(i, _):
        for r in range(2):
            j = 2 * i + r

            def write(ref, place):
                x_sel[j] = ref[place]

            select_tile(tile[j], xs, write)
        rows = x_sel[pl.ds(2 * i, 2)]
        rows = rows.reshape(2 * rows.shape[1], rows.shape[2])
        pre = jnp.dot(rows, w_in[...], preferred_element_type=F32) + bias[...]
        gate = sigmoid(pre)
        hidden = (pre * gate).astype(BF16)
        rise = (gate * (1.0 + pre * (1.0 - gate))).astype(BF16)
        for r in range(2):
            j = 2 * i + r
            slope[j] = rise[r * 128 : (r + 1) * 128]
            term = jnp.dot(adj[j], hidden[r * 128 : (r + 1) * 128], preferred_element_type=F32)
            part[slot[j]] += term
        return 0

    lax.fori_loop(0, count // 2, step, 0, unroll=2)
    for a in range(NX):
        outs[a][...] = part[a * NZ : (a + 1) * NZ, :, :HALF].astype(BF16)
    for r in range(NZ):
        for a in range(NX):
            outs[NX + r][a] = part[a * NZ + lax.rem(me[0] + r, NZ), :, HALF:].astype(BF16)


def edge_forward(me, tile, slot, xs, adj, w_in, bias):
    count, rows, width = adj.shape[0], xs[0].shape[1], xs[0].shape[2]
    block = jax.ShapeDtypeStruct((count, rows, width), BF16)
    by_x = jax.ShapeDtypeStruct((NZ, rows, HALF), BF16)
    by_z = jax.ShapeDtypeStruct((NX, rows, width - HALF), BF16)
    return pl.pallas_call(
        edge_forward_kernel,
        out_shape=(block, block) + (by_x,) * NX + (by_z,) * NZ,
        in_specs=[SMEM] * 3 + [VMEM] * (len(xs) + 3),
        out_specs=(VMEM,) * (2 + NX + NZ),
        scratch_shapes=[pltpu.VMEM((GRID_N, rows, width), F32)],
        compiler_params=kernel_params(28),
        name="edge_forward",
    )(me, tile, slot, *xs, adj, w_in, bias.reshape(1, -1))


def times_transposed(a, b):
    return lax.dot_general(a, b, (((1,), (1,)), ((), ())), preferred_element_type=F32)


def transposed_times(a, b):
    return lax.dot_general(a, b, (((0,), (0,)), ((), ())), preferred_element_type=F32)


def node_kernel(
    agg_a, b0, b1, b2, b3, mesh_lat, cot, w_out, w_node, gain, mesh_out, u_a, u_b, active_out, agg_out, d_agg_out
):
    first = agg_a[0].astype(F32)
    for z in range(1, NZ):
        first += agg_a[z].astype(F32)
    second = b0[...].astype(F32)
    for ref in (b1, b2, b3):
        second += ref[...].astype(F32)
    agg = jnp.concatenate([first, second], axis=1)
    high = agg.astype(BF16)
    low = (agg - high.astype(F32)).astype(BF16)
    aggregate = jnp.dot(high, w_out[...], preferred_element_type=F32) + jnp.dot(
        low, w_out[...], preferred_element_type=F32
    )
    summed = mesh_lat[...].astype(F32) + aggregate
    centred = summed - jnp.mean(summed, axis=-1, keepdims=True)
    inverse = lax.rsqrt(jnp.mean(centred * centred, axis=-1, keepdims=True) + EPSILON)
    standard = centred * inverse
    normed = standard * gain[...]
    gate = sigmoid(normed)
    active = (normed * gate).astype(BF16)
    mesh_out[...] = (summed + jnp.dot(active, w_node[...], preferred_element_type=F32)).astype(BF16)
    d_active = times_transposed(cot[...], w_node[...])
    d_standard = d_active * (gate * (1.0 + normed * (1.0 - gate))) * gain[...]
    first = jnp.mean(d_standard, axis=-1, keepdims=True)
    second = jnp.mean(d_standard * standard, axis=-1, keepdims=True)
    d_summed = cot[...].astype(F32) + inverse * (d_standard - first - standard * second)
    d_agg = d_summed.astype(BF16)
    u = times_transposed(d_agg, w_out[...]).astype(BF16)
    for z in range(NZ):
        u_a[z] = u[:, :HALF]
    u_b[...] = u[:, HALF:]
    active_out[...] = active
    agg_out[...] = high
    d_agg_out[...] = d_agg


def node_step(agg_a, agg_b, mesh_lat, cot, w_out, w_node, gain):
    rows, width = mesh_lat.shape
    whole = jax.ShapeDtypeStruct((rows, width), BF16)
    return pl.pallas_call(
        node_kernel,
        out_shape=(
            whole,
            jax.ShapeDtypeStruct((NZ, rows, HALF), BF16),
            jax.ShapeDtypeStruct((rows, width - HALF), BF16),
            whole,
            whole,
            whole,
        ),
        in_specs=[VMEM] * 10,
        out_specs=(VMEM,) * 6,
        compiler_params=kernel_params(12),
        name="node_step",
    )(agg_a, *agg_b, mesh_lat, cot, w_out, w_node, gain.reshape(1, -1))


def edge_backward_kernel(slot, flipped, out_place, *refs):
    refs, outs, (u_first, u_second, back) = refs[: -MESH_N - 3], refs[-MESH_N - 3 : -3], refs[-3:]
    *refs, adj, slope, d_pre = refs
    for scratch, pieces in ((u_first, refs[:-NZ]), (u_second, refs[-NZ:])):
        start = 0
        for ref in pieces:
            scratch[start : start + ref.shape[0]] = ref[...]
            start += ref.shape[0]

    def step(j, _):
        u = jnp.concatenate([u_first[slot[j]], u_second[flipped[j]]], axis=1)
        term = (transposed_times(adj[j], u) * slope[j].astype(F32)).astype(BF16)
        d_pre[j] = term
        back[out_place[j]] = term
        return 0

    lax.fori_loop(0, adj.shape[0], step, 0, unroll=4)
    for i, ref in enumerate(outs):
        ref[...] = back[4 * i : 4 * (i + 1)]


def edge_backward(slot, flipped, out_place, u_a, u_b, adj, slope):
    count, rows, width = slope.shape
    return pl.pallas_call(
        edge_backward_kernel,
        out_shape=(jax.ShapeDtypeStruct(slope.shape, BF16),)
        + (jax.ShapeDtypeStruct((4, rows, width), BF16),) * MESH_N,
        in_specs=[SMEM] * 3 + [VMEM] * (len(u_a) + len(u_b) + 2),
        out_specs=(VMEM,) * (1 + MESH_N),
        scratch_shapes=[
            pltpu.VMEM((GRID_N, rows, HALF), BF16),
            pltpu.VMEM((GRID_N, rows, width - HALF), BF16),
            pltpu.VMEM((4 * MESH_N, rows, width), BF16),
        ],
        compiler_params=kernel_params(26),
        name="edge_backward",
    )(slot, flipped, out_place, *u_a, *u_b, adj, slope)


def row_kernel(place, *refs):
    parts = refs[:MESH_N]
    w_in, out, acc = refs[MESH_N:]
    acc[...] = jnp.zeros_like(acc)
    for s, ref in enumerate(parts):
        for q in range(4):

            @pl.when(place[s * 4 + q] >= 0)
            def _():
                acc[place[s * 4 + q]] += ref[q].astype(F32)

    blocks, rows, width = acc.shape
    for i in range(0, blocks, 2):
        row_sum = acc[i : i + 2].reshape(2 * rows, width).astype(BF16)
        out[i * rows : (i + 2) * rows] = times_transposed(row_sum, w_in[...]).astype(BF16)


def row_step(place, parts, w_in, blocks):
    _, rows, width = parts[0].shape
    return pl.pallas_call(
        row_kernel,
        out_shape=jax.ShapeDtypeStruct((blocks * rows, width), BF16),
        in_specs=[SMEM] + [VMEM] * (MESH_N + 1),
        out_specs=VMEM,
        scratch_shapes=[pltpu.VMEM((blocks, rows, width), F32)],
        compiler_params=kernel_params(16),
        name="row_step",
    )(place, *parts, w_in)


def pick(v, index):
    return lax.dynamic_index_in_dim(v, index, 0, keepdims=False)


def fold_kernel(me, keep, got, *outs):
    for k, out in enumerate(outs):
        y = lax.rem(me[0] + k, NY)
        out[...] = (keep[y].astype(F32) + got[y].astype(F32)).astype(BF16)


def reduce_core(v, my_y, my_core):
    rows, width = v.shape
    v = v.reshape(NY, 2, rows // MESH_N, width)
    keep = lax.dynamic_index_in_dim(v, my_core, 1, keepdims=False)
    got = send_y(lax.dynamic_index_in_dim(v, 1 - my_core, 1, keepdims=False), 0, 1)
    return pl.pallas_call(
        fold_kernel,
        out_shape=(jax.ShapeDtypeStruct((rows // MESH_N, width), BF16),) * NY,
        in_specs=[SMEM, VMEM, VMEM],
        out_specs=(VMEM,) * NY,
        compiler_params=kernel_params(8),
        name="fold",
    )(my_y.reshape(1), keep, got)


def shares_kernel(*refs):
    *parts, out = refs
    count, run, _ = out.shape
    t = parts[0][...].astype(F32)
    for p in parts[1:]:
        t = t + p[...].astype(F32)
    for i in range(count):
        out[i] = t[i * run : (i + 1) * run].astype(BF16)


def reduce_y(parts):
    rows, width = parts[0].shape
    parts = [parts[0]] + [send_y(parts[k], k, 0) for k in (2, 1, 3)]
    return pl.pallas_call(
        shares_kernel,
        out_shape=jax.ShapeDtypeStruct((GRID_N, rows // GRID_N, width), BF16),
        in_specs=[VMEM] * NY,
        out_specs=VMEM,
        compiler_params=kernel_params(8),
        name="shares",
    )(*parts)


def reduce_grid(v):
    return lax.all_to_all(v, "grid", 0, 0).astype(F32).sum(0).astype(BF16)


def spread_grid(v):
    rows, width = v.shape
    v = lax.all_to_all(jnp.broadcast_to(v[None], (GRID_N, rows, width)), "grid", 0, 0)
    return v.reshape(GRID_N * rows, width)


def spread_y(v):
    return jnp.stack([v] + [send_y(v, -k, 0) for k in (1, 2, 3)])


def finish_kernel(scales, me, mine, other, *outs):
    run = mine.shape[1]
    width = outs[0].shape[1]
    for k in range(NY):
        y = lax.rem(me[0] + k, NY)
        for ref, core in ((mine, me[1]), (other, 1 - me[1])):
            rows = pl.ds(pl.multiple_of((2 * y + core) * run, run), run)
            for i, out in enumerate(outs):
                out[rows, :] = ref[k, :, i * width : (i + 1) * width].astype(F32) * scales[i]


def finish(me, mine, other, width, scales):
    return pl.pallas_call(
        lambda *refs: finish_kernel(scales, *refs),
        out_shape=(jax.ShapeDtypeStruct((width, width), F32),) * 3,
        in_specs=[SMEM, VMEM, VMEM],
        out_specs=(VMEM,) * 3,
        compiler_params=kernel_params(12),
        name="finish",
    )(me, mine, other)


def shards(
    grid_lat,
    mesh_lat,
    edge_grid_block,
    edge_mesh_block,
    edge_sender,
    edge_receiver,
    edge_live,
    weight_in,
    bias_in,
    weight_out,
    norm_gain,
    weight_node,
    cotangent,
):
    block_rows, width = mesh_lat.shape
    local_blocks = grid_lat.shape[0] // block_rows
    edge_blocks = edge_grid_block.shape[0]
    slot_count = edge_sender.shape[0] // edge_blocks
    g, m = lax.axis_index("grid"), lax.axis_index("mesh")
    my_x, my_z, my_y, my_core = g // NZ, g % NZ, m // 2, m % 2

    holder, place = edge_grid_block // local_blocks, edge_grid_block % local_blocks
    rel_holder = ((holder // 2 - my_y) % NY) * 2 + ((holder % 2) ^ my_core)
    tile = rel_holder * local_blocks + place
    rel_x, rel_z = (edge_mesh_block // NZ - my_x) % NX, (edge_mesh_block % NZ - my_z) % NZ
    slot, flipped = rel_x * NZ + edge_mesh_block % NZ, rel_z * NX + rel_x
    earlier = jnp.arange(edge_blocks)[None, :] < jnp.arange(edge_blocks)[:, None]
    rank = jnp.sum((rel_holder[:, None] == rel_holder[None, :]) & earlier, axis=1).astype(jnp.int32)
    out_place = rel_holder * 4 + rank

    own = grid_lat.reshape(local_blocks, block_rows, width)
    half = local_blocks // 2
    after, before = send_y(own, -1), send_y(own, 1)
    far = [send_y(before[:half], 1), send_y(after[half:], -1)]
    other_own, blocks = order_together(send_y(own, 0, 1), edge_grid_block)

    table = jnp.stack([blocks] + [send_y(blocks, -k, 0) for k in (1, 2, 3)])
    table = jnp.stack([table, send_y(table, 0, 1)], axis=1).reshape(MESH_N, edge_blocks)
    mine = (table // local_blocks == m)[:, :, None]
    order = jnp.cumsum(mine.astype(jnp.int32), axis=1) - 1
    hit = mine & (order == jnp.arange(4, dtype=jnp.int32))
    returned = jnp.sum(jnp.where(hit, (table % local_blocks)[:, :, None] + 1, 0), axis=1) - 1
    returned = returned.reshape(-1)

    sender = edge_sender.reshape(edge_blocks, slot_count)
    receiver = edge_receiver.reshape(edge_blocks, slot_count)
    lanes = jnp.arange(block_rows, dtype=jnp.int32)
    live = jnp.arange(slot_count, dtype=jnp.int32)[None, :] < edge_live[:, None]
    send_hot = (sender[:, :, None] == lanes).astype(BF16)
    receive_hot = ((receiver[:, :, None] == lanes) & live[:, :, None]).astype(BF16)
    adj = jnp.einsum("ker,ket->krt", receive_hot, send_hot, preferred_element_type=F32).astype(BF16)

    after, adj, tile, slot, flipped, out_place, returned = order_together(
        after, adj, tile, slot, flipped, out_place, returned
    )
    xs = [own, other_own, after, send_y(after, 0, 1), *far]
    xs += [*(send_y(v, 0, 1) for v in far), before, send_y(before, 0, 1)]

    x_sel, slope, *parts = edge_forward(my_z.reshape(1), tile, slot, xs, adj, weight_in, bias_in)

    z_sums = scatter_z_ring(parts[NX:])
    x_sums = scatter_x_twice(parts[:NX])
    agg_a = exchange_z(x_sums)
    agg_b = [z_sums[0]] + [send_x(z_sums[k], k) for k in (1, 3, 2)]

    mesh_out, u_a, u_b, active, agg, d_agg = node_step(
        agg_a, agg_b, mesh_lat, cotangent, weight_out, weight_node, norm_gain
    )
    u_b = jnp.stack([u_b] + [send_x(u_b, -k) for k in range(1, NX)])
    u_a = exchange_z(u_a)
    u_a = gather_x_twice(u_a)
    u_b = gather_z_ring(u_b)

    d_pre, *back = edge_backward(slot, flipped, out_place, u_a, u_b, adj, slope)

    in_term = transposed_times(
        x_sel.reshape(edge_blocks * block_rows, width), d_pre.reshape(edge_blocks * block_rows, width)
    )
    node_term, out_term = transposed_times(active, cotangent), transposed_times(agg, d_agg)
    sums = jnp.concatenate([in_term, out_term, node_term], axis=1).astype(BF16)

    got = [back[0]] + [None] * (MESH_N - 1)
    for k in (0, 2, 1, 3):
        for c in range(2):
            if k or c:
                got[((NY - k) % NY) * 2 + c] = send_y(back[k * 2 + c], k, c)
    sums = reduce_core(sums, my_y, my_core)
    sums = reduce_y(sums)
    sums = reduce_grid(sums)
    sums, got[1], got[4], got[5] = order_together(sums, got[1], got[4], got[5])
    sums = spread_grid(sums)
    sums, got[6], got[2] = order_together(sums, got[6], got[2])
    sums = spread_y(sums)
    sums, got[7], got[3] = order_together(sums, got[7], got[3])
    others = send_y(sums, 0, 1)

    grid_grad = row_step(returned, got, weight_in, local_blocks)

    by_edge = 1.0 / math.sqrt(edge_blocks * slot_count * GRID_N * MESH_N)
    by_node = 1.0 / math.sqrt(block_rows * GRID_N * MESH_N)
    me = jnp.stack([my_y, my_core]).astype(jnp.int32)
    grad_in, grad_out, grad_node = finish(me, sums, others, width, (by_edge, by_edge, by_node))
    return (mesh_out, grid_grad, grad_in, grad_out, grad_node)


def solution(mesh):
    rows = P(("grid", "mesh"), None)
    line = P(("grid", "mesh"))
    return jax.shard_map(
        shards,
        mesh=mesh,
        in_specs=(rows, rows, line, line, line, line, line, P(), P(), P(), P(), P(), rows),
        out_specs=(rows, rows, P(), P(), P()),
        check_vma=False,
    )
```
